256 devices in a mesh: clus: 64 (over z, x, core), pair: 4 (over y).
Axes of the slice: x: 4, y: 4, z: 8, core: 2. Of those that a mesh axis runs over, the one named last changes fastest.
Arguments:
- right_side: float32 [8, 65536], P(None, 'clus'), as said below
- start: float32 [8, 65536], P(None, 'clus'), may hold values from -3 to 3
- cluster_sizes: int32 [256], P('clus'), may hold values from 1 to 256, 49152 in all
- self_blocks: bfloat16 [256, 256, 256], P(('clus', 'pair')), as said below
- near_blocks: bfloat16 [4096, 256, 256], P(('clus', 'pair')), may hold values from -0.25 to 0.25
- near_pairs: int32 [4096, 2], P(('clus', 'pair')), may hold values from 0 to 11, as said below
- far_factors: bfloat16 [16384, 2, 24, 256], P(('clus', 'pair')), may hold values from -0.25 to 0.25
- far_group: int32 [16384, 1], P(('clus', 'pair')), may hold values from 0 to 63; in each aligned block of 64 rows (0 to 63, 64 to 127, ...) at most 2 rows name the same one
- far_local: int32 [16384, 2], P(('clus', 'pair')), may hold values from 0 to 3
- block_counts: int32 [256, 2], P(('clus', 'pair')), may hold values from 1 to 64, as said below
Outputs:
- next_iterate: float32 [8, 65536], P(None, 'clus')
- next_basis: float32 [8, 65536], P(None, 'clus')
- residual_norm: float32 [8], replicated
The draws below stay inside these ranges and needn't reach their ends.
Inputs may be any that keep to these rules, and one draw needn't show every extreme that they name: `right_side`: custom float draw of the right-hand sides. `self_blocks`: each self block is symmetric. `near_pairs`: A row (a, c) on a device of clus index g names cluster g * 4 + a and cluster (g - 1) * 4 + c; c never equals 4 + a, and both clusters exist. `far_group`: at most 2 of the rows of one device name one group, and some device reaches 2. `block_counts`: column 0 counts live near slots and column 1 live far slots of each device; the other slots are padding. Some device has 16 live near slots and some device 64 live far slots.
All inputs are finite; a program needn't handle non-finite values. No bound on the sum of `cluster_sizes` on one device may be relied on, other than what follows from the above.
Results may differ from the reference program's by a relative error of at most 0.004.
Values may be sent and summed in bfloat16 or wider, within the bound.
A program may use at most 64 MiB of HBM per device.

```python
import math
import jax
import jax.numpy as jnp
import numpy as np
from jax import lax

PAD = 256
RANK = 24
RHS = 8
CG = 4
NEAR_PER = 16
CLUSTERS = 256
PANELS = 65536
NEAR_DEV = 16
FAR_DEV = 64
NEAR_PAIRS = 4096
FAR_PAIRS = 16384
CAP = 2
N_CLUS = 64


def draw_right_side(key, part):
    key = jax.random.fold_in(key, 5)
    first = jax.random.fold_in(key, 0)
    ramp = 1.0 + 2.0 * jnp.arange(PANELS, dtype=jnp.float32) / PANELS
    noise = jax.random.truncated_normal(first, -6.0, 6.0, (RHS, PANELS), jnp.float32)
    return ramp * noise


def draw_self_blocks(key, part):
    key = jax.random.fold_in(key, 7)
    scale = 0.5 / PAD ** 0.5
    noise = jax.random.truncated_normal(key, -6.0, 6.0, (CLUSTERS, PAD, PAD), jnp.float32)
    symmetric = (noise + jnp.swapaxes(noise, 1, 2)) * (0.7071 * scale)
    return (symmetric + 2.0 * jnp.eye(PAD, dtype=jnp.float32)[None]).astype(jnp.bfloat16)


def draw_near_pairs(key, part):
    key = jax.random.fold_in(key, 11)
    first, second = jax.random.split(key)
    rows = jnp.arange(NEAR_PAIRS, dtype=jnp.int32)
    pair_count = NEAR_PER * CG // NEAR_DEV
    groups = CLUSTERS // CG
    group_index = rows // NEAR_DEV // pair_count
    own_member = jax.random.randint(first, (NEAR_PAIRS,), 0, CG, dtype=jnp.int32)
    lower = jnp.where(group_index == 0, CG, 0)
    upper = jnp.where(group_index == groups - 1, 2 * CG, 3 * CG)
    raw = jax.random.randint(second, (NEAR_PAIRS,), 0, 1 << 20, dtype=jnp.int32)
    column = lower + raw % (upper - lower - 1)
    column = jnp.where(column >= CG + own_member, column + 1, column)
    return jnp.stack([own_member, column], axis=1).astype(jnp.int32)


def draw_block_counts(key, part):
    key = jax.random.fold_in(key, 13)
    first, second, third, fourth = jax.random.split(key, 4)
    device_count = NEAR_PAIRS // NEAR_DEV
    near_live = jax.random.randint(first, (device_count,), 1, NEAR_DEV + 1, dtype=jnp.int32)
    far_live = jax.random.randint(second, (device_count,), 1, FAR_DEV + 1, dtype=jnp.int32)
    near_live = near_live.at[jax.random.randint(third, (), 0, device_count, dtype=jnp.int32)].set(NEAR_DEV)
    far_live = far_live.at[jax.random.randint(fourth, (), 0, device_count, dtype=jnp.int32)].set(FAR_DEV)
    return jnp.stack([near_live, far_live], axis=1).astype(jnp.int32)


def set_ends(array, key, smallest, high):
    extent = array.shape
    spot = [jax.random.randint(jax.random.fold_in(key, axis), (), 0, extent[axis]) for axis in range(len(extent))]
    array = array.at[tuple(spot)].set(smallest)
    longest = extent.index(max(extent))
    spot[longest] = (spot[longest] + 1) % extent[longest]
    return array.at[tuple(spot)].set(high)


def shard_levels(stream_key, shape, shards, least, high):
    def one(dim, shards_of):
        heights = jax.random.uniform(jax.random.fold_in(jax.random.fold_in(stream_key, 6), dim), (shards_of,), jnp.float32, least / len(shards), high / len(shards))
        return jnp.repeat(jnp.exp(heights), shape[dim] // shards_of).reshape((-1,) + (1,) * (len(shape) - dim - 1))

    loudness = one(*shards[0])
    for cut in shards[1:]:
        loudness = loudness * one(*cut)
    return loudness


def length_profile(count, total, most, skew):
    loads = [(1 << 20) // math.isqrt(standing ** skew) + 1 for standing in range(2, count + 1)]
    spare, given = total - most - (count - 1), [1] * (count - 1)
    while spare > 0:
        free = [i for i in range(count - 1) if given[i] < most]
        mass, budget = sum([loads[i] for i in free]), spare
        for i in free:
            more = min(most - given[i], max(1, budget * loads[i] // mass), spare)
            given[i] = given[i] + more
            spare = spare - more
    return np.array([most] + given)


def uneven_parts(rng, amount, total, reach, lean):
    if amount == 2:
        one = jax.random.randint(rng, (), max(1, total - reach), min(reach, total - 1) + 1)
        return jnp.stack([one, total - one])
    sizes = jnp.asarray(length_profile(amount, total, reach, lean), jnp.int32)
    couples = (amount - 1) // 2
    source_of, sink = sizes[1:1 + 2 * couples:2], sizes[2:2 + 2 * couples:2]
    room = jnp.minimum(source_of - 1, reach - sink)
    shifted = jax.random.randint(jax.random.fold_in(rng, 1), (couples,), 0, 1 << 20) % (room + 1)
    sizes = sizes.at[1:1 + 2 * couples:2].set(source_of - shifted).at[2:2 + 2 * couples:2].set(sink + shifted)
    return sizes[jax.random.permutation(jax.random.fold_in(rng, 2), amount)]


def assign_block(stream_key, own, number, rows, count, top, most, skew):
    ranking = jax.random.permutation(stream_key, count)
    crowded, ordinary = shares(count, rows * top, most, skew, True), shares(count, rows * top, most, skew, False)
    places = jnp.arange(count)

    def named(tallies, rotation):
        used = int((tallies > 0).sum())
        fixed = max(1, used // 4)
        shifted = fixed + (places - fixed + rotation * (used - fixed)) % max(1, count - fixed)
        return jnp.zeros((count,), jnp.int32).at[ranking[jnp.where(places < fixed, places, shifted)]].set(jnp.asarray(tallies, jnp.int32))

    tallies = jnp.where(number % 4 == 0, named(crowded, number // 4), named(ordinary, number - number // 4 - 1))
    mixed = jax.random.permutation(jax.random.fold_in(own, 3), count)
    donor, receiver = mixed[0:count // 2 * 2:2], mixed[1:count // 2 * 2:2]
    slack = jnp.minimum(tallies[donor] - 1, most - tallies[receiver]) // 2
    slack = jnp.where((donor == ranking[0]) | (receiver == ranking[0]) | (tallies[receiver] == 0), 0, jnp.maximum(slack, 0))
    shifted = jax.random.randint(jax.random.fold_in(own, 4), (count // 2,), 0, 1 << 20) % (slack + 1)
    tallies = tallies.at[donor].add(-shifted).at[receiver].add(shifted)
    labels = jnp.searchsorted(jnp.cumsum(tallies), jnp.arange(rows * top), side="right").astype(jnp.int32)
    listing = labels.reshape(top, rows).T
    listing = listing[jax.random.permutation(jax.random.fold_in(own, 1), rows)]
    rotation = jax.random.randint(jax.random.fold_in(own, 2), (rows, 1), 0, top)
    return jnp.take_along_axis(listing, (jnp.arange(top)[None, :] + rotation) % top, axis=1)


def shares(count, total, limit, lean, full):
    weights = [(1 << 20) // math.isqrt(standing ** lean) + 1 for standing in range(1, count + 1)]
    largest = limit if full else min(limit, max(-(-total // count), total * weights[0] // sum(weights)))
    least = 1 if total - largest >= count - 1 else 0
    holding, rest = [largest] + [least] * (count - 1), total - largest - least * (count - 1)
    while rest > 0:
        candidates = [i for i in range(1, count) if holding[i] < largest] or [i for i in range(1, count) if holding[i] < limit]
        pool, remaining = sum([weights[i] for i in candidates]), rest
        for i in candidates:
            more = min(limit - holding[i], max(1, remaining * weights[i] // pool), rest)
            holding[i] = holding[i] + more
            rest = rest - more
    return np.array(holding)


def gaussian(stream_key, extent, deviation, limit, pieces=(), kind=jnp.bfloat16):
    drawn = deviation * jax.random.normal(stream_key, extent, jnp.float32)
    if pieces:
        drawn = drawn * shard_levels(stream_key, extent, pieces, -0.22, 0.18)
    return jnp.clip(drawn, -limit, limit).astype(kind)


def setup_inputs(seed: int = 0) -> dict:
    keys = jax.random.split(jax.random.key(seed), 11)
    right_side = draw_right_side(jax.random.fold_in(keys[10], 71), 0)
    start = gaussian(keys[1], (RHS, PANELS), 0.5, 3.0, ((1, 64),), jnp.float32)
    cluster_sizes = uneven_parts(keys[2], CLUSTERS, CLUSTERS * PAD * 3 // 4, PAD, 1).astype(jnp.int32)
    self_blocks = draw_self_blocks(jax.random.fold_in(keys[10], 71), 0)
    near_blocks = gaussian(keys[4], (NEAR_PAIRS, PAD, PAD), (2 * PAD) ** -0.5, 0.25, ((0, 256),))
    near_pairs = draw_near_pairs(jax.random.fold_in(keys[10], 71), 0)
    far_factors = gaussian(keys[6], (FAR_PAIRS, 2, RANK, PAD), (2 * PAD) ** -0.5, 0.25, ((0, 256),))
    far_group_keys = jax.random.split(jax.random.fold_in(keys[7], 1), FAR_PAIRS // FAR_DEV)
    far_group_turns = jax.random.permutation(jax.random.fold_in(keys[7], 3), FAR_PAIRS // FAR_DEV)
    far_group = jax.vmap(lambda own, number: assign_block(jax.random.fold_in(keys[7], 2), own, number, FAR_DEV, N_CLUS, 1, CAP, 1))(far_group_keys, far_group_turns).reshape((FAR_PAIRS, 1))
    far_local = set_ends(jax.random.randint(keys[8], (FAR_PAIRS, 2), 0, CG), jax.random.fold_in(keys[8], 1), 0, CG - 1).astype(jnp.int32)
    block_counts = draw_block_counts(jax.random.fold_in(keys[10], 71), 0)
    return {"right_side": right_side, "start": start, "cluster_sizes": cluster_sizes, "self_blocks": self_blocks, "near_blocks": near_blocks, "near_pairs": near_pairs, "far_factors": far_factors, "far_group": far_group, "far_local": far_local, "block_counts": block_counts}


epsilon = 1e-06

def panel_mask(cluster_sizes):
    return (jnp.arange(PAD, dtype=jnp.int32)[None, :] < cluster_sizes[:, None]).astype(jnp.float32)

def round_trip(values):
    return lax.optimization_barrier(values.astype(jnp.bfloat16)).astype(jnp.float32)

def apply_operator(vector, valid, self_blocks, near_blocks, near_pairs, far_factors, far_group, far_local, block_counts):
    packed = round_trip(vector * valid[None])
    result = jnp.einsum('cab,qcb->qca', self_blocks.astype(jnp.float32), packed)
    device_count = NEAR_PAIRS // NEAR_DEV
    pair_count = device_count // (CLUSTERS // CG)

    def near_step(total, device):
        blocks = lax.dynamic_slice_in_dim(near_blocks, device * NEAR_DEV, NEAR_DEV, 0).astype(jnp.float32)
        pair_rows = lax.dynamic_slice_in_dim(near_pairs, device * NEAR_DEV, NEAR_DEV, 0)
        group_index = device // pair_count
        rows = (group_index * CG + pair_rows[:, 0]).astype(jnp.int32)
        columns = ((group_index - 1) * CG + pair_rows[:, 1]).astype(jnp.int32)
        active = (jnp.arange(NEAR_DEV, dtype=jnp.int32) < block_counts[device, 0]).astype(jnp.float32)[None, :, None]
        forward = jnp.einsum('kab,qkb->qka', blocks, packed[:, columns]) * active
        backward = jnp.einsum('kab,qka->qkb', blocks, packed[:, rows]) * active
        return (total.at[:, rows].add(forward).at[:, columns].add(backward), None)
    result = lax.scan(near_step, result, jnp.arange(device_count, dtype=jnp.int32))[0]

    def far_step(total, device):
        factors = lax.dynamic_slice_in_dim(far_factors, device * FAR_DEV, FAR_DEV, 0).astype(jnp.float32)
        local_rows = lax.dynamic_slice_in_dim(far_local, device * FAR_DEV, FAR_DEV, 0)
        targets = lax.dynamic_slice_in_dim(far_group, device * FAR_DEV, FAR_DEV, 0)
        group_index = device // pair_count
        rows = (group_index * CG + local_rows[:, 0]).astype(jnp.int32)
        columns = (targets[:, 0] * CG + local_rows[:, 1]).astype(jnp.int32)
        active = (jnp.arange(FAR_DEV, dtype=jnp.int32) < block_counts[device, 1]).astype(jnp.float32)[None, :, None]
        left_side = factors[:, 0]
        right_side = factors[:, 1]
        coefficients = round_trip(jnp.einsum('krp,qkp->qkr', right_side, packed[:, columns]))
        toward_rows = jnp.einsum('krp,qkr->qkp', left_side, coefficients) * active
        coef_back = round_trip(jnp.einsum('krp,qkp->qkr', left_side, packed[:, rows]))
        toward_columns = jnp.einsum('krp,qkr->qkp', right_side, coef_back) * active
        return (total.at[:, rows].add(toward_rows).at[:, columns].add(toward_columns), None)
    result = lax.scan(far_step, result, jnp.arange(device_count, dtype=jnp.int32))[0]
    return result * valid[None]

def reference(right_side, start, cluster_sizes, self_blocks, near_blocks, near_pairs, far_factors, far_group, far_local, block_counts):
    valid = panel_mask(cluster_sizes)

    def operator(vector):
        return apply_operator(vector, valid, self_blocks, near_blocks, near_pairs, far_factors, far_group, far_local, block_counts)
    source = right_side.reshape(RHS, CLUSTERS, PAD) * valid[None]
    initial = start.reshape(RHS, CLUSTERS, PAD) * valid[None]
    residual = source - operator(initial)
    mean_square = lax.optimization_barrier(jnp.sum(residual * residual, axis=(1, 2))) / PANELS
    start_norm = jnp.sqrt(mean_square + epsilon)
    basis = residual / start_norm[:, None, None]
    image = operator(basis)
    h_diag = lax.optimization_barrier(jnp.sum(basis * image, axis=(1, 2))) / PANELS
    remainder = image - h_diag[:, None, None] * basis
    h_below = jnp.sqrt(lax.optimization_barrier(jnp.sum(remainder * remainder, axis=(1, 2))) / PANELS + epsilon)
    denominator = h_diag * h_diag + h_below * h_below
    step_size = start_norm * h_diag / denominator
    next_iterate = initial + step_size[:, None, None] * basis
    next_basis = remainder / h_below[:, None, None]
    residual_norm = start_norm * h_below / jnp.sqrt(denominator)
    return (next_iterate.reshape(RHS, PANELS), next_basis.reshape(RHS, PANELS), residual_norm)
```

```python
import functools

import jax
import jax.numpy as jnp
from jax import lax
from jax.experimental import pallas as pl
from jax.experimental.pallas import tpu as pltpu
from jax.sharding import PartitionSpec as P

PAD = 256
RHS = 8
CG = 4
RANK = 24
NZ, NX, NC, NY = 8, 4, 2, 4
GROUPS = NZ * NX * NC
PANELS = GROUPS * CG * PAD
NEAR = 16
FAR = 64
CHUNK = 16
CHUNKS = FAR // CHUNK
WIDE = CHUNK * RANK
BLOCK = NZ * CG

EPSILON = 1e-06
F32 = jnp.float32
BF16 = jnp.bfloat16

AT_COUNTS = 0
AT_NEAR_ROW = 2
AT_NEAR_COL = AT_NEAR_ROW + NEAR
AT_GROUP = AT_NEAR_COL + NEAR
AT_LOCAL_ROW = AT_GROUP + FAR
AT_LOCAL_COL = AT_LOCAL_ROW + FAR
AT_SIZES = AT_LOCAL_COL + FAR


def fold(tile):
    return jnp.concatenate([tile[..., :128], tile[..., 128:]], axis=-2)


def unfold(tile):
    return jnp.concatenate([tile[..., :RHS, :], tile[..., RHS:, :]], axis=-1)


def dot_nt(a, b):
    return lax.dot_general(a, b, (((1,), (1,)), ((), ())), preferred_element_type=F32)


def dot_nn(a, b):
    return lax.dot_general(a, b, (((1,), (0,)), ((), ())), preferred_element_type=F32)


def ratio(a, n):
    ok = n > 1e-30
    return jnp.where(ok, a / jnp.where(ok, n, 1.0), 0.0)


def about(a, n, s, centre):
    own = ratio(a, n)
    off = own - centre
    return s + 2.0 * off * (a - own * n) + off * off * n


def merge(parts):
    a = functools.reduce(lambda p, q: p + q, [part[0] for part in parts])
    n = functools.reduce(lambda p, q: p + q, [part[1] for part in parts])
    centre = ratio(a, n)
    s = functools.reduce(lambda p, q: p + q, [about(*part, centre) for part in parts])
    return a, n, s


def kernel(
    ids,
    rhs_ref,
    start_ref,
    self_hbm,
    near_hbm,
    far_hbm,
    iterate_ref,
    basis_ref,
    norm_ref,
    self_blk,
    near_blk,
    far_raw,
    left_all,
    right_all,
    onehot,
    row_of,
    field_first,
    field_second,
    own_field,
    far_back,
    near_back,
    spread,
    core_in,
    x_out,
    x_in,
    z_out,
    z_in,
    y_buf,
    resid,
    stat_z,
    stat_xc,
    load_sem,
    send_sem,
    agz_sem,
    agx_sem,
    agc_sem,
    rsc_sem,
    rsx_sem,
    rsz_sem,
    y_sem,
    stz_sem,
    stx_sem,
):
    me = lax.axis_index("clus")
    y = lax.axis_index("pair")
    z, x, c = me // (NX * NC), (me // NC) % NX, me % NC

    def dev(zz=None, xx=None, cc=None, yy=None):
        zz = z if zz is None else zz
        xx = x if xx is None else xx
        cc = c if cc is None else cc
        yy = y if yy is None else yy
        return ((zz * NX + xx) * NC + cc, yy)

    def send(src, dst, ssem, rsem, target):
        pltpu.make_async_remote_copy(
            src_ref=src,
            dst_ref=dst,
            send_sem=ssem,
            recv_sem=rsem,
            device_id=target,
            device_id_type=pl.DeviceIdType.MESH,
        ).start()

    def await_bytes(ref, sem):
        pltpu.make_async_copy(ref, ref, sem).wait()

    z_targets = [dev(zz=(z + d) % NZ) for d in range(1, NZ)]
    x_others = [(x + d) % NX for d in range(1, NX)]
    x_targets = [dev(xx=o) for o in x_others]
    y_targets = [dev(yy=(y + d) % NY) for d in range(1, NY)]
    core = dev(cc=1 - c)
    cross = [dev(xx=o, cc=1 - c) for o in x_others]
    xc_targets = x_targets + [core] + cross
    partners = z_targets + y_targets + xc_targets

    loads = [
        pltpu.make_async_copy(far_hbm, far_raw, load_sem.at[0]),
        pltpu.make_async_copy(near_hbm, near_blk, load_sem.at[1]),
        pltpu.make_async_copy(self_hbm, self_blk, load_sem.at[2]),
    ]
    for load in loads:
        load.start()

    barrier = pltpu.get_barrier_semaphore()
    for target in partners:
        pl.semaphore_signal(
            barrier, inc=1, device_id=target, device_id_type=pl.DeviceIdType.MESH
        )

    lane = lax.broadcasted_iota(jnp.int32, (RHS, PAD), 1)
    valid = [(lane < ids[AT_SIZES + i]).astype(F32) for i in range(CG)]
    near_live = ids[AT_COUNTS]
    far_live = ids[AT_COUNTS + 1]

    own_block = c * NX + x
    own_base = (own_block * NZ + z) * CG

    def base_of(group):
        return (((group % NC) * NX + (group // NC) % NX) * NZ + group // (NX * NC)) * CG

    below = (me + GROUPS - 1) % GROUPS
    above = (me + 1) % GROUPS
    below_base = base_of(below)
    above_base = base_of(above)
    below_x = (below // NC) % NX
    above_x = (above // NC) % NX

    def far_place(k):
        group = ids[AT_GROUP + k]
        block = lax.bitwise_and(group, 1) * NX + lax.bitwise_and(
            lax.shift_right_logical(group, 1), 3
        )
        return (block * NZ + lax.shift_right_logical(group, 3)) * CG + ids[AT_LOCAL_COL + k]

    diagonal = (
        lax.broadcasted_iota(jnp.int32, (CHUNK * RHS, WIDE), 0) // RHS
        == lax.broadcasted_iota(jnp.int32, (CHUNK * RHS, WIDE), 1) // RANK
    )

    def prepare():
        slot = lax.broadcasted_iota(jnp.int32, (RHS, WIDE), 1) // RANK

        def rows_step(chunk, carry):
            table = jnp.full((RHS, WIDE), -1, jnp.int32)
            for s in range(CHUNK):
                k = chunk * CHUNK + s
                row = jnp.where(k < far_live, ids[AT_LOCAL_ROW + k], -1)
                table = jnp.where(slot == s, row, table)
            row_of[chunk] = table
            return carry

        lax.fori_loop(0, CHUNKS, rows_step, 0)

        wide = lax.broadcasted_iota(jnp.int32, (RHS, FAR * RHS), 1)

        def place_step(k, table):
            return jnp.where(wide // RHS == k, far_place(k), table)

        table = lax.fori_loop(
            0, FAR, place_step, jnp.full((RHS, FAR * RHS), -1, jnp.int32)
        )
        same = lax.broadcasted_iota(jnp.int32, (RHS, FAR * RHS), 0) == wide % RHS
        table = jnp.where(same, table, -1)

        def onehot_step(i, carry):
            two = jnp.concatenate(
                [
                    jnp.where(table == 2 * i, 1.0, 0.0),
                    jnp.where(table == 2 * i + 1, 1.0, 0.0),
                ],
                axis=0,
            ).astype(BF16)
            onehot[pl.ds(pl.multiple_of(i * 16, 16), 16), :] = two
            return carry

        lax.fori_loop(0, GROUPS * CG // 2, onehot_step, 0)
        loads[0].wait()

        def factor_step(chunk, carry):
            rows = pl.ds(pl.multiple_of(chunk * WIDE, WIDE), WIDE)
            raw = far_raw[pl.ds(chunk * CHUNK, CHUNK)].astype(F32)
            left_all[rows, :] = raw[:, 0].reshape(WIDE, PAD).astype(BF16)
            right_all[rows, :] = raw[:, 1].reshape(WIDE, PAD).astype(BF16)
            return carry

        lax.fori_loop(0, CHUNKS, factor_step, 0)

    def apply_operator(a, values):
        field = (field_first, field_second)[a]
        for i in range(CG):
            packed = values[i].astype(BF16).astype(F32)
            own_field[a, i] = packed
            field[own_base + i] = fold(packed).astype(BF16)
        if a == 0:
            pl.semaphore_wait(barrier, len(partners))
        mine = field.at[pl.ds(own_base, CG)]
        for target in z_targets:
            send(mine, mine, send_sem.at[a, 0], agz_sem.at[a], target)

        if a == 0:
            prepare()

        own_rows = jnp.concatenate([own_field[a, i] for i in range(CG)], axis=0).astype(BF16)

        def back_step(chunk, carry):
            rows = pl.ds(pl.multiple_of(chunk * WIDE, WIDE), WIDE)
            every = dot_nt(own_rows, left_all[rows, :])
            table = row_of[chunk]
            coef = jnp.zeros((RHS, WIDE), F32)
            for i in range(CG):
                coef = coef + jnp.where(table == i, every[i * RHS : (i + 1) * RHS], 0.0)
            tall = jnp.concatenate([coef] * CHUNK, axis=0)
            tall = jnp.where(diagonal, tall, 0.0).astype(BF16)
            out = dot_nn(tall, right_all[rows, :])
            far_back[a, pl.ds(pl.multiple_of(chunk * CHUNK * RHS, CHUNK * RHS), CHUNK * RHS), :] = (
                out.astype(BF16)
            )
            return carry

        lax.fori_loop(0, CHUNKS, back_step, 0)

        if a == 0:
            loads[1].wait()
            loads[2].wait()
        near_back[a] = jnp.zeros((3 * CG, RHS, PAD), F32)

        def near_back_step(k, carry):
            live = jnp.where(k < near_live, 1.0, 0.0)
            out = dot_nn(own_field[a, ids[AT_NEAR_ROW + k]].astype(BF16), near_blk[k])
            column = ids[AT_NEAR_COL + k]
            for j in range(3 * CG):
                near_back[a, j] += out * jnp.where(column == j, live, 0.0)
            return carry

        lax.fori_loop(0, NEAR, near_back_step, 0)

        def spread_chunk(block):
            rows = pl.ds(pl.multiple_of(block * BLOCK * RHS, BLOCK * RHS), BLOCK * RHS)
            out = dot_nn(onehot[rows, :], far_back[a])
            return fold(out.reshape(BLOCK, RHS, PAD))

        def theirs_step(o, carry):
            block = (1 - c) * NX + o
            spread[a, o] = spread_chunk(block).astype(BF16)
            for side_x, side_base, first in (
                (below_x, below_base, 0),
                (above_x, above_base, 2 * CG),
            ):

                @pl.when(side_x == o)
                def _():
                    at = side_base - block * BLOCK
                    for i in range(CG):
                        spread[a, o, at + i] = (
                            spread[a, o, at + i].astype(F32) + fold(near_back[a, first + i])
                        ).astype(BF16)

            send(
                spread.at[a, o], core_in.at[a, o], send_sem.at[a, 1], rsc_sem.at[a, o], core
            )
            return carry

        lax.fori_loop(0, NX, theirs_step, 0)

        await_bytes(field.at[pl.ds(0, CG * (NZ - 1))], agz_sem.at[a])
        whole = field.at[pl.ds(own_block * BLOCK, BLOCK)]
        for d, target in enumerate(x_targets):
            send(whole, whole, send_sem.at[a, 2], agx_sem.at[a, d], target)
        send(whole, whole, send_sem.at[a, 3], agc_sem.at[a], core)

        def ours_step(d, carry):
            o = (x + d) % NX
            await_bytes(core_in.at[a, o], rsc_sem.at[a, o])
            total = spread_chunk(c * NX + o) + core_in[a, o].astype(F32)
            x_out[a, o] = total.astype(BF16)

            @pl.when(d < NX)
            def _():
                send(
                    x_out.at[a, o], x_in.at[a, x], send_sem.at[a, 4], rsx_sem.at[a], dev(xx=o)
                )

            return carry

        lax.fori_loop(1, NX + 1, ours_step, 0)

        for d in range(1, NX):
            o = (x + NX - d) % NX
            came = field.at[pl.ds((c * NX + o) * BLOCK, BLOCK)]
            await_bytes(came, agx_sem.at[a, d - 1])
            send(came, came, send_sem.at[a, 3], agc_sem.at[a], core)

        await_bytes(x_in.at[a, pl.ds(0, NX - 1)], rsx_sem.at[a])
        x_in[a, x] = x_out[a, x]

        def x_sum_step(o, carry):
            tiles = pl.ds(o * CG, CG)
            total = x_in[a, 0, tiles].astype(F32)
            for j in range(1, NX):
                total = total + x_in[a, j, tiles].astype(F32)
            z_out[a, o] = total.astype(BF16)
            return carry

        lax.fori_loop(0, NZ, x_sum_step, 0)
        for d in range(1, NZ):
            o = (z + d) % NZ
            send(z_out.at[a, o], z_in.at[a, z], send_sem.at[a, 5], rsz_sem.at[a], dev(zz=o))

        await_bytes(field.at[pl.ds(0, GROUPS * CG // 2)], agc_sem.at[a])

        def near_step(k, sums):
            column = ids[AT_NEAR_COL + k]
            base = jnp.where(
                column < CG, below_base, jnp.where(column < 2 * CG, own_base, above_base)
            )
            tile = unfold(field[base + lax.bitwise_and(column, CG - 1)].astype(F32))
            out = dot_nt(tile.astype(BF16), near_blk[k])
            row = ids[AT_NEAR_ROW + k]
            live = jnp.where(k < near_live, 1.0, 0.0)
            return tuple(
                sums[i] + out * jnp.where(row == i, live, 0.0) for i in range(CG)
            )

        sums = tuple(near_back[a, CG + i] for i in range(CG))
        sums = lax.fori_loop(0, NEAR, near_step, sums)

        def forth_step(chunk, total):
            rows = pl.ds(pl.multiple_of(chunk * WIDE, WIDE), WIDE)
            tiles = [
                unfold(field[far_place(chunk * CHUNK + s)].astype(F32))
                for s in range(CHUNK)
            ]
            tall = jnp.concatenate(tiles, axis=0).astype(BF16)
            every = jnp.where(diagonal, dot_nt(tall, right_all[rows, :]), 0.0)
            coef = jnp.sum(every.reshape(CHUNK, RHS, WIDE), axis=0)
            table = row_of[chunk]
            four = jnp.concatenate(
                [jnp.where(table == i, coef, 0.0) for i in range(CG)], axis=0
            )
            return total + dot_nn(four.astype(BF16), left_all[rows, :])

        far_rows = lax.fori_loop(0, CHUNKS, forth_step, jnp.zeros((CG * RHS, PAD), F32))
        self_out = dot_nt(own_field[a, y].astype(BF16), self_blk[0])

        await_bytes(z_in.at[a, pl.ds(0, NZ - 1)], rsz_sem.at[a])
        z_in[a, z] = z_out[a, z]
        for i in range(CG):
            total = sums[i] + far_rows[i * RHS : (i + 1) * RHS]
            total = total + self_out * jnp.where(y == i, 1.0, 0.0)
            come = z_in[a, 0, i].astype(F32)
            for j in range(1, NZ):
                come = come + z_in[a, j, i].astype(F32)
            y_buf[a, y, i] = total + unfold(come)
        for target in y_targets:
            send(y_buf.at[a, y], y_buf.at[a, y], send_sem.at[a, 6], y_sem.at[a], target)
        await_bytes(y_buf.at[a, pl.ds(0, NY - 1)], y_sem.at[a])
        return [
            valid[i] * (y_buf[a, 0, i] + y_buf[a, 1, i] + y_buf[a, 2, i] + y_buf[a, 3, i])
            for i in range(CG)
        ]

    def share_z(s, planes):
        for p, plane in enumerate(planes):
            stat_z[s, z, p] = jnp.broadcast_to(plane, (RHS, 128))
        part = stat_z.at[s, z]
        for target in z_targets:
            send(part, part, send_sem.at[s, 7], stz_sem.at[s], target)

    def share_xc(s, planes):
        for p, plane in enumerate(planes):
            stat_xc[s, own_block, p] = plane
        part = stat_xc.at[s, own_block]
        for target in xc_targets:
            send(part, part, send_sem.at[s, 8], stx_sem.at[s], target)

    def total_of(tiles):
        return jnp.sum(
            functools.reduce(lambda p, q: p + q, tiles), axis=1, keepdims=True
        )

    def cut(ref, i):
        return ref[:, i * PAD : (i + 1) * PAD]

    initial = [cut(start_ref, i) * valid[i] for i in range(CG)]
    image = apply_operator(0, initial)
    for i in range(CG):
        resid[i] = cut(rhs_ref, i) * valid[i] - image[i]

    zero = jnp.zeros((RHS, 1), F32)
    share_z(0, [total_of([resid[i] * resid[i] for i in range(CG)]), zero, zero])
    image = apply_operator(1, [resid[i] for i in range(CG)])

    await_bytes(stat_z.at[0, pl.ds(0, NZ - 1)], stz_sem.at[0])
    square = stat_z[0, 0, 0]
    for j in range(1, NZ):
        square = square + stat_z[0, j, 0]
    share_xc(0, [square, jnp.zeros((RHS, 128), F32), jnp.zeros((RHS, 128), F32)])
    await_bytes(stat_xc.at[0, pl.ds(0, NX * NC - 1)], stx_sem.at[0])
    square = stat_xc[0, 0, 0]
    for j in range(1, NX * NC):
        square = square + stat_xc[0, j, 0]
    start_norm = jnp.sqrt(square / PANELS + EPSILON)
    wide_norm = jnp.concatenate([start_norm, start_norm], axis=1)

    basis = [resid[i] / wide_norm for i in range(CG)]
    image = [image[i] / wide_norm for i in range(CG)]
    inner = total_of([basis[i] * image[i] for i in range(CG)])
    size = total_of([basis[i] * basis[i] for i in range(CG)])
    centre = ratio(inner, size)
    rest = [image[i] - centre * basis[i] for i in range(CG)]
    share_z(1, [inner, size, total_of([rest[i] * rest[i] for i in range(CG)])])
    await_bytes(stat_z.at[1, pl.ds(0, NZ - 1)], stz_sem.at[1])
    merged = merge([tuple(stat_z[1, j, p] for p in range(3)) for j in range(NZ)])
    share_xc(1, merged)
    await_bytes(stat_xc.at[1, pl.ds(0, NX * NC - 1)], stx_sem.at[1])
    merged = merge([tuple(stat_xc[1, j, p] for p in range(3)) for j in range(NX * NC)])

    h_diag = merged[0] / PANELS
    below_square = jnp.maximum(about(*merged, h_diag), 0.0) / PANELS
    h_below = jnp.sqrt(below_square + EPSILON)
    denominator = h_diag * h_diag + h_below * h_below
    step_size = start_norm * h_diag / denominator
    residual_norm = start_norm * h_below / jnp.sqrt(denominator)
    wide = lambda tile: jnp.concatenate([tile, tile], axis=1)
    for i in range(CG):
        iterate_ref[:, i * PAD : (i + 1) * PAD] = (
            cut(start_ref, i) * valid[i] + wide(step_size) * basis[i]
        )
        basis_ref[:, i * PAD : (i + 1) * PAD] = (
            image[i] - wide(h_diag) * basis[i]
        ) / wide(h_below)
    pick = lax.broadcasted_iota(jnp.int32, (RHS, 128), 0) == lax.broadcasted_iota(
        jnp.int32, (RHS, 128), 1
    )
    norm_ref[...] = jnp.sum(jnp.where(pick, residual_norm, 0.0), axis=0, keepdims=True)

    for a in range(2):
        field = (field_first, field_second)[a]
        tiles = field.at[pl.ds(0, CG * (NZ - 1))]
        await_bytes(tiles, send_sem.at[a, 0])
        await_bytes(spread.at[a], send_sem.at[a, 1])
        await_bytes(field.at[pl.ds(0, BLOCK * (NX - 1))], send_sem.at[a, 2])
        await_bytes(field.at[pl.ds(0, BLOCK * NX)], send_sem.at[a, 3])
        await_bytes(x_in.at[a, pl.ds(0, NX - 1)], send_sem.at[a, 4])
        await_bytes(z_in.at[a, pl.ds(0, NZ - 1)], send_sem.at[a, 5])
        await_bytes(y_buf.at[a, pl.ds(0, NY - 1)], send_sem.at[a, 6])
        await_bytes(stat_z.at[a, pl.ds(0, NZ - 1)], send_sem.at[a, 7])
        await_bytes(stat_xc.at[a, pl.ds(0, NX * NC - 1)], send_sem.at[a, 8])


def local(
    right_side,
    start,
    cluster_sizes,
    self_blocks,
    near_blocks,
    near_pairs,
    far_factors,
    far_group,
    far_local,
    block_counts,
):
    ids = jnp.concatenate(
        [
            block_counts[0],
            near_pairs[:, 0],
            near_pairs[:, 1],
            far_group[:, 0],
            far_local[:, 0],
            far_local[:, 1],
            cluster_sizes,
        ]
    )
    vmem = pl.BlockSpec(memory_space=pltpu.VMEM)
    hbm = pl.BlockSpec(memory_space=pl.ANY)
    dma = pltpu.SemaphoreType.DMA
    wide = (RHS, CG * PAD)
    iterate, basis, norm = pl.pallas_call(
        kernel,
        out_shape=(
            jax.ShapeDtypeStruct(wide, F32),
            jax.ShapeDtypeStruct(wide, F32),
            jax.ShapeDtypeStruct((1, 128), F32),
        ),
        in_specs=[pl.BlockSpec(memory_space=pltpu.SMEM), vmem, vmem, hbm, hbm, hbm],
        out_specs=(vmem, vmem, vmem),
        scratch_shapes=[
            pltpu.VMEM((1, PAD, PAD), BF16),
            pltpu.VMEM((NEAR, PAD, PAD), BF16),
            pltpu.VMEM((FAR, 2, RANK, PAD), BF16),
            pltpu.VMEM((FAR * RANK, PAD), BF16),
            pltpu.VMEM((FAR * RANK, PAD), BF16),
            pltpu.VMEM((GROUPS * CG * RHS, FAR * RHS), BF16),
            pltpu.VMEM((CHUNKS, RHS, WIDE), jnp.int32),
            pltpu.VMEM((GROUPS * CG, 16, 128), BF16),
            pltpu.VMEM((GROUPS * CG, 16, 128), BF16),
            pltpu.VMEM((2, CG, RHS, PAD), F32),
            pltpu.VMEM((2, FAR * RHS, PAD), BF16),
            pltpu.VMEM((2, 3 * CG, RHS, PAD), F32),
            pltpu.VMEM((2, NX, BLOCK, 16, 128), BF16),
            pltpu.VMEM((2, NX, BLOCK, 16, 128), BF16),
            pltpu.VMEM((2, NX, BLOCK, 16, 128), BF16),
            pltpu.VMEM((2, NX, BLOCK, 16, 128), BF16),
            pltpu.VMEM((2, NZ, CG, 16, 128), BF16),
            pltpu.VMEM((2, NZ, CG, 16, 128), BF16),
            pltpu.VMEM((2, NY, CG, RHS, PAD), F32),
            pltpu.VMEM((CG, RHS, PAD), F32),
            pltpu.VMEM((2, NZ, 3, RHS, 128), F32),
            pltpu.VMEM((2, NX * NC, 3, RHS, 128), F32),
            dma((3,)),
            dma((2, 9)),
            dma((2,)),
            dma((2, NX - 1)),
            dma((2,)),
            dma((2, NX)),
            dma((2,)),
            dma((2,)),
            dma((2,)),
            dma((2,)),
            dma((2,)),
        ],
        compiler_params=pltpu.CompilerParams(
            collective_id=0, has_side_effects=True, vmem_limit_bytes=48 * 1024 * 1024
        ),
    )(ids, right_side, start, self_blocks, near_blocks, far_factors)
    return iterate, basis, norm[0, :RHS]


def solution(mesh):
    in_specs = (
        P(None, "clus"),
        P(None, "clus"),
        P("clus"),
        P(("clus", "pair"), None, None),
        P(("clus", "pair"), None, None),
        P(("clus", "pair"), None),
        P(("clus", "pair"), None, None, None),
        P(("clus", "pair"), None),
        P(("clus", "pair"), None),
        P(("clus", "pair"), None),
    )
    out_specs = (P(None, "clus"), P(None, "clus"), P())
    return jax.shard_map(local, mesh=mesh, in_specs=in_specs, out_specs=out_specs, check_vma=False)
```

```python
import functools

import jax
import jax.numpy as jnp
from jax import lax
from jax.experimental import pallas as pl
from jax.experimental.pallas import tpu as pltpu
from jax.sharding import PartitionSpec as P

PAD = 256
RHS = 8
CG = 4
RANK = 24
NZ, NX, NC, NY = 8, 4, 2, 4
GROUPS = NZ * NX * NC
PANELS = GROUPS * CG * PAD
NEAR = 16
FAR = 64
CHUNK = 16
CHUNKS = FAR // CHUNK
WIDE = CHUNK * RANK
HALF = NZ * NX * CG
PART = NX * CG
UNROLL = 8

EPSILON = 1e-06
F32 = jnp.float32
BF16 = jnp.bfloat16

def fold(tile):
    return jnp.concatenate([tile[..., :128], tile[..., 128:]], axis=-2)


def unfold(tile):
    return jnp.concatenate([tile[..., :RHS, :], tile[..., RHS:, :]], axis=-1)


def dot_nt(a, b):
    return lax.dot_general(a, b, (((1,), (1,)), ((), ())), preferred_element_type=F32)


def dot_nn(a, b):
    return lax.dot_general(a, b, (((1,), (0,)), ((), ())), preferred_element_type=F32)


def ratio(a, n):
    ok = n > 1e-30
    return jnp.where(ok, a / jnp.where(ok, n, 1.0), 0.0)


def about(a, n, s, centre):
    own = ratio(a, n)
    off = own - centre
    return s + 2.0 * off * (a - own * n) + off * off * n


def merge(parts):
    a = functools.reduce(lambda p, q: p + q, [part[0] for part in parts])
    n = functools.reduce(lambda p, q: p + q, [part[1] for part in parts])
    centre = ratio(a, n)
    s = functools.reduce(lambda p, q: p + q, [about(*part, centre) for part in parts])
    return a, n, s


def kernel(
    counts_hbm,
    pairs_hbm,
    group_hbm,
    local_hbm,
    sizes_hbm,
    rhs_hbm,
    start_hbm,
    self_hbm,
    near_hbm,
    far_hbm,
    iterate_ref,
    basis_ref,
    norm_ref,
    counts,
    pairs,
    groups,
    locals_,
    sizes,
    rhs_ref,
    start_ref,
    self_blk,
    near_blk,
    far_raw,
    left_all,
    right_all,
    onehot,
    row_of,
    field_first,
    field_second,
    own_field,
    far_back,
    near_back,
    spread,
    core_in,
    x_out,
    x_in,
    z_out,
    z_in,
    y_buf,
    resid,
    stat_z,
    stat_xc,
    load_sem,
    send_sem,
    agz_sem,
    agx_sem,
    agc_sem,
    rsc_sem,
    rsx_sem,
    rsz_sem,
    y_sem,
    stz_sem,
    stx_sem,
):
    me = lax.axis_index("clus")
    y = lax.axis_index("pair")
    z, x, c = me // (NX * NC), (me // NC) % NX, me % NC

    loads = [
        pltpu.make_async_copy(src, dst, load_sem.at[i])
        for i, (src, dst) in enumerate(
            [
                (counts_hbm, counts),
                (pairs_hbm, pairs),
                (group_hbm, groups),
                (local_hbm, locals_),
                (sizes_hbm, sizes),
                (start_hbm, start_ref),
                (far_hbm, far_raw),
                (near_hbm, near_blk),
                (self_hbm, self_blk),
                (rhs_hbm, rhs_ref),
            ]
        )
    ]
    for load in loads:
        load.start()

    def dev(zz=None, xx=None, cc=None, yy=None):
        zz = z if zz is None else zz
        xx = x if xx is None else xx
        cc = c if cc is None else cc
        yy = y if yy is None else yy
        return ((zz * NX + xx) * NC + cc, yy)

    def send(src, dst, ssem, rsem, target):
        pltpu.make_async_remote_copy(
            src_ref=src,
            dst_ref=dst,
            send_sem=ssem,
            recv_sem=rsem,
            device_id=target,
            device_id_type=pl.DeviceIdType.MESH,
        ).start()

    def await_bytes(ref, sem):
        pltpu.make_async_copy(ref, ref, sem).wait()

    z_targets = [dev(zz=(z + d) % NZ) for d in range(1, NZ)]
    x_others = [(x + d) % NX for d in range(1, NX)]
    x_targets = [dev(xx=o) for o in x_others]
    y_targets = [dev(yy=(y + d) % NY) for d in range(1, NY)]
    core = dev(cc=1 - c)
    cross = [dev(xx=o, cc=1 - c) for o in x_others]
    xc_targets = x_targets + [core] + cross
    partners = z_targets + y_targets + xc_targets

    barrier = pltpu.get_barrier_semaphore()
    for target in partners:
        pl.semaphore_signal(
            barrier, inc=1, device_id=target, device_id_type=pl.DeviceIdType.MESH
        )

    for load in loads[:6]:
        load.wait()
    lane = lax.broadcasted_iota(jnp.int32, (RHS, PAD), 1)
    valid = [(lane < sizes[i]).astype(F32) for i in range(CG)]
    near_live = counts[0, 0]
    far_live = counts[0, 1]

    def base_of(group):
        return (group % NC) * HALF + (group // NC) * CG

    own_base = base_of(me)
    below = (me + GROUPS - 1) % GROUPS
    above = (me + 1) % GROUPS
    below_base = base_of(below)
    above_base = base_of(above)

    def far_place(k):
        group = groups[0, k]
        return (
            lax.bitwise_and(group, 1) * HALF
            + lax.shift_right_logical(group, 1) * CG
            + locals_[1, k]
        )

    diagonal = (
        lax.broadcasted_iota(jnp.int32, (CHUNK * RHS, WIDE), 0) // RHS
        == lax.broadcasted_iota(jnp.int32, (CHUNK * RHS, WIDE), 1) // RANK
    )

    def far_to_near(j):
        odd = j % 2
        return (z + NZ // 2 + (1 - 2 * odd) * ((j + 1) // 2)) % NZ

    def prepare():
        slot = lax.broadcasted_iota(jnp.int32, (RHS, WIDE), 1) // RANK

        def rows_step(chunk, carry):
            table = jnp.full((RHS, WIDE), -1, jnp.int32)
            for s in range(CHUNK):
                k = chunk * CHUNK + s
                row = jnp.where(k < far_live, locals_[0, k], -1)
                table = jnp.where(slot == s, row, table)
            row_of[chunk] = table
            return carry

        lax.fori_loop(0, CHUNKS, rows_step, 0)

        wide = lax.broadcasted_iota(jnp.int32, (RHS, FAR * RHS), 1)
        slot_of = wide // RHS

        def place_step(step, table):
            for s in range(8):
                k = step * 8 + s
                table = jnp.where(slot_of == k, far_place(k), table)
            return table

        table = lax.fori_loop(
            0, FAR // 8, place_step, jnp.full((RHS, FAR * RHS), -1, jnp.int32)
        )
        same = lax.broadcasted_iota(jnp.int32, (RHS, FAR * RHS), 0) == wide % RHS
        table = jnp.where(same, table, -1)

        def onehot_step(step, carry):
            for s in range(4):
                i = step * 4 + s
                two = jnp.concatenate(
                    [
                        jnp.where(table == 2 * i, 1.0, 0.0),
                        jnp.where(table == 2 * i + 1, 1.0, 0.0),
                    ],
                    axis=0,
                ).astype(BF16)
                onehot[pl.ds(pl.multiple_of(i * 16, 16), 16), :] = two
            return carry

        lax.fori_loop(0, GROUPS * CG // 8, onehot_step, 0)
        loads[6].wait()

        def factor_step(chunk, carry):
            rows = pl.ds(pl.multiple_of(chunk * WIDE, WIDE), WIDE)
            raw = far_raw[pl.ds(chunk * CHUNK, CHUNK)].astype(F32)
            left_all[rows, :] = raw[:, 0].reshape(WIDE, PAD).astype(BF16)
            right_all[rows, :] = raw[:, 1].reshape(WIDE, PAD).astype(BF16)
            return carry

        lax.fori_loop(0, CHUNKS, factor_step, 0)

    def apply_operator(a, values):
        field = (field_first, field_second)[a]
        for i in range(CG):
            packed = values[i].astype(BF16).astype(F32)
            low = values[i] - packed if a else jnp.zeros_like(packed)
            own_field[a, i] = jnp.concatenate([packed, low], axis=0)
            field[own_base + i] = fold(packed).astype(BF16)
        mine = field.at[pl.ds(own_base, CG)]

        def send_field():
            for d, target in enumerate(z_targets):
                send(mine, mine, send_sem.at[a, 0], agz_sem.at[a, d], target)
            for target in x_targets:
                send(mine, mine, send_sem.at[a, 2], agx_sem.at[a, z], target)

        def far_out():
            own_rows = jnp.concatenate(
                [own_field[a, i, 0:RHS] for i in range(CG)], axis=0
            ).astype(BF16)

            def back_step(chunk, carry):
                rows = pl.ds(pl.multiple_of(chunk * WIDE, WIDE), WIDE)
                every = dot_nt(own_rows, left_all[rows, :])
                table = row_of[chunk]
                coef = jnp.zeros((RHS, WIDE), F32)
                for i in range(CG):
                    coef = coef + jnp.where(
                        table == i, every[i * RHS : (i + 1) * RHS], 0.0
                    )
                tall = jnp.concatenate([coef] * CHUNK, axis=0)
                tall = jnp.where(diagonal, tall, 0.0).astype(BF16)
                out = dot_nn(tall, right_all[rows, :])
                at = pl.ds(pl.multiple_of(chunk * CHUNK * RHS, CHUNK * RHS), CHUNK * RHS)
                far_back[a, at, :] = out.astype(BF16)
                return carry

            lax.fori_loop(0, CHUNKS, back_step, 0, unroll=True)

        def near_out():
            near_back[a] = jnp.zeros((3 * CG, RHS, PAD), F32)

            def near_back_step(step, carry):
                for s in range(UNROLL):
                    k = step * UNROLL + s
                    live = jnp.where(k < near_live, 1.0, 0.0)
                    out = dot_nn(own_field[a, pairs[0, k]].astype(BF16), near_blk[k])
                    out = out[:RHS] + out[RHS:]
                    column = pairs[1, k]
                    for j in range(3 * CG):
                        near_back[a, j] += out * jnp.where(column == j, live, 0.0)
                return carry

            lax.fori_loop(0, NEAR // UNROLL, near_back_step, 0)

        def spread_part(half, zz):
            block = half * NZ + zz
            rows = pl.ds(pl.multiple_of(block * PART * RHS, PART * RHS), PART * RHS)
            out = dot_nn(onehot[rows, :], far_back[a])
            return fold(out.reshape(PART, RHS, PAD))

        def theirs_step(j, carry):
            zz = far_to_near(j)
            spread[a, zz] = spread_part(1 - c, zz).astype(BF16)
            return carry

        def beside_step(j, carry):
            zz = far_to_near(j)
            for base, first in ((below_base, 0), (above_base, 2 * CG)):
                at = base % HALF

                @pl.when(at // PART == zz)
                def _():
                    for i in range(CG):
                        spread[a, zz, at % PART + i] = (
                            spread[a, zz, at % PART + i].astype(F32)
                            + fold(near_back[a, first + i])
                        ).astype(BF16)

            return carry

        def to_core_step(j, carry):
            zz = far_to_near(j)
            send(
                spread.at[a, zz], core_in.at[a, zz], send_sem.at[a, 1], rsc_sem.at[a, zz], core
            )
            return carry

        def ours_step(j, carry):
            zz = far_to_near(j)
            await_bytes(core_in.at[a, zz], rsc_sem.at[a, zz])
            total = spread_part(c, zz) + core_in[a, zz].astype(F32)
            x_out[a, zz] = total.reshape(NX, CG, 16, 128).astype(BF16)
            for o in x_others:
                send(
                    x_out.at[a, zz, o],
                    x_in.at[a, zz, x],
                    send_sem.at[a, 4],
                    rsx_sem.at[a, zz],
                    dev(xx=o),
                )
            return carry

        def pass_along_x(offsets):
            for d in offsets:
                zz = (z + NZ - d) % NZ
                came = field.at[pl.ds(base_of((zz * NX + x) * NC + c), CG)]
                await_bytes(came, agz_sem.at[a, d - 1])
                for target in x_targets:
                    send(came, came, send_sem.at[a, 2], agx_sem.at[a, zz], target)

        if a == 0:
            prepare()
            far_out()
            pl.semaphore_wait(barrier, len(partners))
            send_field()
        else:
            send_field()
            far_out()

        def both(j, carry):
            return to_core_step(j, theirs_step(j, carry))

        lax.fori_loop(0, NZ - 3, both, 0)
        if a == 0:
            loads[7].wait()
            loads[8].wait()
        near_out()

        def all_three(j, carry):
            return to_core_step(j, beside_step(j, theirs_step(j, carry)))

        lax.fori_loop(NZ - 3, NZ, all_three, 0)
        pass_along_x([1, 7])
        lax.fori_loop(0, NZ, ours_step, 0)
        pass_along_x([2, 6, 3, 5, 4])

        def x_sum_step(j, carry):
            zz = far_to_near(j)
            await_bytes(x_in.at[a, zz, pl.ds(0, NX - 1)], rsx_sem.at[a, zz])
            x_in[a, zz, x] = x_out[a, zz, x]
            total = x_in[a, zz, 0].astype(F32)
            for o in range(1, NX):
                total = total + x_in[a, zz, o].astype(F32)
            z_out[a, zz] = total.astype(BF16)

            @pl.when(j < NZ - 1)
            def _():
                send(
                    z_out.at[a, zz], z_in.at[a, z], send_sem.at[a, 5], rsz_sem.at[a], dev(zz=zz)
                )

            return carry

        lax.fori_loop(0, NZ, x_sum_step, 0)

        def to_core_field(d, carry):
            zz = (z + d) % NZ
            slab = field.at[pl.ds(c * HALF + zz * PART, PART)]
            await_bytes(field.at[pl.ds(0, PART - CG)], agx_sem.at[a, zz])
            send(slab, slab, send_sem.at[a, 3], agc_sem.at[a], core)
            return carry

        lax.fori_loop(0, NZ, to_core_field, 0)

        await_bytes(field.at[pl.ds(0, HALF)], agc_sem.at[a])

        def near_step(step, sums):
            for s in range(UNROLL):
                k = step * UNROLL + s
                column = pairs[1, k]
                inside = lax.bitwise_and(column, CG - 1)
                own = jnp.logical_and(column >= CG, column < 2 * CG)
                base = jnp.where(column < CG, below_base, jnp.where(own, own_base, above_base))
                tile = unfold(field[base + inside].astype(F32))
                low = own_field[a, inside, RHS:] * jnp.where(own, 1.0, 0.0)
                tile = jnp.concatenate([tile, low], axis=0).astype(BF16)
                out = dot_nt(tile, near_blk[k])
                out = out[:RHS] + out[RHS:]
                row = pairs[0, k]
                live = jnp.where(k < near_live, 1.0, 0.0)
                sums = tuple(
                    sums[i] + out * jnp.where(row == i, live, 0.0) for i in range(CG)
                )
            return sums

        sums = tuple(near_back[a, CG + i] for i in range(CG))
        sums = lax.fori_loop(0, NEAR // UNROLL, near_step, sums)

        def forth_step(chunk, total):
            rows = pl.ds(pl.multiple_of(chunk * WIDE, WIDE), WIDE)
            tiles = [
                unfold(field[far_place(chunk * CHUNK + s)].astype(F32))
                for s in range(CHUNK)
            ]
            tall = jnp.concatenate(tiles, axis=0).astype(BF16)
            every = jnp.where(diagonal, dot_nt(tall, right_all[rows, :]), 0.0)
            coef = jnp.sum(every.reshape(CHUNK, RHS, WIDE), axis=0)
            table = row_of[chunk]
            four = jnp.concatenate(
                [jnp.where(table == i, coef, 0.0) for i in range(CG)], axis=0
            )
            return total + dot_nn(four.astype(BF16), left_all[rows, :])

        far_rows = lax.fori_loop(
            0, CHUNKS, forth_step, jnp.zeros((CG * RHS, PAD), F32), unroll=True
        )
        self_out = dot_nt(own_field[a, y].astype(BF16), self_blk[0])
        self_out = self_out[:RHS] + self_out[RHS:]

        await_bytes(z_in.at[a, pl.ds(0, NZ - 1)], rsz_sem.at[a])
        z_in[a, z] = z_out[a, z]
        for i in range(CG):
            total = sums[i] + far_rows[i * RHS : (i + 1) * RHS]
            total = total + self_out * jnp.where(y == i, 1.0, 0.0)
            come = z_in[a, 0, i].astype(F32)
            for j in range(1, NZ):
                come = come + z_in[a, j, i].astype(F32)
            y_buf[a, y, i] = total + unfold(come)
        for target in y_targets:
            send(y_buf.at[a, y], y_buf.at[a, y], send_sem.at[a, 6], y_sem.at[a], target)
        await_bytes(y_buf.at[a, pl.ds(0, NY - 1)], y_sem.at[a])
        return [
            valid[i] * (y_buf[a, 0, i] + y_buf[a, 1, i] + y_buf[a, 2, i] + y_buf[a, 3, i])
            for i in range(CG)
        ]

    def share_z(s, planes):
        for p, plane in enumerate(planes):
            stat_z[s, z, p] = jnp.broadcast_to(plane, (RHS, 128))
        part = stat_z.at[s, z]
        for target in z_targets:
            send(part, part, send_sem.at[s, 7], stz_sem.at[s], target)

    def share_xc(s, planes):
        for p, plane in enumerate(planes):
            stat_xc[s, c * NX + x, p] = plane
        part = stat_xc.at[s, c * NX + x]
        for target in xc_targets:
            send(part, part, send_sem.at[s, 8], stx_sem.at[s], target)

    def total_of(tiles):
        return jnp.sum(
            functools.reduce(lambda p, q: p + q, tiles), axis=1, keepdims=True
        )

    def cut(ref, i):
        return ref[:, i * PAD : (i + 1) * PAD]

    initial = [cut(start_ref, i) * valid[i] for i in range(CG)]
    image = apply_operator(0, initial)
    loads[9].wait()
    for i in range(CG):
        resid[i] = cut(rhs_ref, i) * valid[i] - image[i]

    zero = jnp.zeros((RHS, 1), F32)
    share_z(0, [total_of([resid[i] * resid[i] for i in range(CG)]), zero, zero])
    image = apply_operator(1, [resid[i] for i in range(CG)])

    await_bytes(stat_z.at[0, pl.ds(0, NZ - 1)], stz_sem.at[0])
    square = stat_z[0, 0, 0]
    for j in range(1, NZ):
        square = square + stat_z[0, j, 0]
    share_xc(0, [square, jnp.zeros((RHS, 128), F32), jnp.zeros((RHS, 128), F32)])
    await_bytes(stat_xc.at[0, pl.ds(0, NX * NC - 1)], stx_sem.at[0])
    square = stat_xc[0, 0, 0]
    for j in range(1, NX * NC):
        square = square + stat_xc[0, j, 0]
    start_norm = jnp.sqrt(square / PANELS + EPSILON)
    wide_norm = jnp.concatenate([start_norm, start_norm], axis=1)

    basis = [resid[i] / wide_norm for i in range(CG)]
    image = [image[i] / wide_norm for i in range(CG)]
    inner = total_of([basis[i] * image[i] for i in range(CG)])
    size = total_of([basis[i] * basis[i] for i in range(CG)])
    centre = ratio(inner, size)
    rest = [image[i] - centre * basis[i] for i in range(CG)]
    share_z(1, [inner, size, total_of([rest[i] * rest[i] for i in range(CG)])])
    await_bytes(stat_z.at[1, pl.ds(0, NZ - 1)], stz_sem.at[1])
    merged = merge([tuple(stat_z[1, j, p] for p in range(3)) for j in range(NZ)])
    share_xc(1, merged)
    await_bytes(stat_xc.at[1, pl.ds(0, NX * NC - 1)], stx_sem.at[1])
    merged = merge([tuple(stat_xc[1, j, p] for p in range(3)) for j in range(NX * NC)])

    h_diag = merged[0] / PANELS
    below_square = jnp.maximum(about(*merged, h_diag), 0.0) / PANELS
    h_below = jnp.sqrt(below_square + EPSILON)
    denominator = h_diag * h_diag + h_below * h_below
    step_size = start_norm * h_diag / denominator
    residual_norm = start_norm * h_below / jnp.sqrt(denominator)
    wide = lambda tile: jnp.concatenate([tile, tile], axis=1)
    for i in range(CG):
        iterate_ref[:, i * PAD : (i + 1) * PAD] = (
            cut(start_ref, i) * valid[i] + wide(step_size) * basis[i]
        )
        basis_ref[:, i * PAD : (i + 1) * PAD] = (
            image[i] - wide(h_diag) * basis[i]
        ) / wide(h_below)
    pick = lax.broadcasted_iota(jnp.int32, (RHS, 128), 0) == lax.broadcasted_iota(
        jnp.int32, (RHS, 128), 1
    )
    norm_ref[...] = jnp.sum(jnp.where(pick, residual_norm, 0.0), axis=0, keepdims=True)

    for a in range(2):
        field = (field_first, field_second)[a]
        await_bytes(field.at[pl.ds(0, CG * (NZ - 1))], send_sem.at[a, 0])
        await_bytes(spread.at[a], send_sem.at[a, 1])
        await_bytes(field.at[pl.ds(0, NZ * (NX - 1) * CG)], send_sem.at[a, 2])
        await_bytes(field.at[pl.ds(0, HALF)], send_sem.at[a, 3])
        await_bytes(x_in.at[a, pl.ds(0, NZ), pl.ds(0, NX - 1)], send_sem.at[a, 4])
        await_bytes(z_in.at[a, pl.ds(0, NZ - 1)], send_sem.at[a, 5])
        await_bytes(y_buf.at[a, pl.ds(0, NY - 1)], send_sem.at[a, 6])
        await_bytes(stat_z.at[a, pl.ds(0, NZ - 1)], send_sem.at[a, 7])
        await_bytes(stat_xc.at[a, pl.ds(0, NX * NC - 1)], send_sem.at[a, 8])


def local(
    right_side,
    start,
    cluster_sizes,
    self_blocks,
    near_blocks,
    near_pairs,
    far_factors,
    far_group,
    far_local,
    block_counts,
):
    vmem = pl.BlockSpec(memory_space=pltpu.VMEM)
    hbm = pl.BlockSpec(memory_space=pl.ANY)
    dma = pltpu.SemaphoreType.DMA
    wide = (RHS, CG * PAD)
    iterate, basis, norm = pl.pallas_call(
        kernel,
        out_shape=(
            jax.ShapeDtypeStruct(wide, F32),
            jax.ShapeDtypeStruct(wide, F32),
            jax.ShapeDtypeStruct((1, 128), F32),
        ),
        in_specs=[hbm] * 10,
        out_specs=(vmem, vmem, vmem),
        scratch_shapes=[
            pltpu.SMEM((1, 2), jnp.int32),
            pltpu.SMEM((2, NEAR), jnp.int32),
            pltpu.SMEM((1, FAR), jnp.int32),
            pltpu.SMEM((2, FAR), jnp.int32),
            pltpu.SMEM((CG,), jnp.int32),
            pltpu.VMEM(wide, F32),
            pltpu.VMEM(wide, F32),
            pltpu.VMEM((1, PAD, PAD), BF16),
            pltpu.VMEM((NEAR, PAD, PAD), BF16),
            pltpu.VMEM((FAR, 2, RANK, PAD), BF16),
            pltpu.VMEM((FAR * RANK, PAD), BF16),
            pltpu.VMEM((FAR * RANK, PAD), BF16),
            pltpu.VMEM((GROUPS * CG * RHS, FAR * RHS), BF16),
            pltpu.VMEM((CHUNKS, RHS, WIDE), jnp.int32),
            pltpu.VMEM((GROUPS * CG, 16, 128), BF16),
            pltpu.VMEM((GROUPS * CG, 16, 128), BF16),
            pltpu.VMEM((2, CG, 2 * RHS, PAD), F32),
            pltpu.VMEM((2, FAR * RHS, PAD), BF16),
            pltpu.VMEM((2, 3 * CG, RHS, PAD), F32),
            pltpu.VMEM((2, NZ, PART, 16, 128), BF16),
            pltpu.VMEM((2, NZ, PART, 16, 128), BF16),
            pltpu.VMEM((2, NZ, NX, CG, 16, 128), BF16),
            pltpu.VMEM((2, NZ, NX, CG, 16, 128), BF16),
            pltpu.VMEM((2, NZ, CG, 16, 128), BF16),
            pltpu.VMEM((2, NZ, CG, 16, 128), BF16),
            pltpu.VMEM((2, NY, CG, RHS, PAD), F32),
            pltpu.VMEM((CG, RHS, PAD), F32),
            pltpu.VMEM((2, NZ, 3, RHS, 128), F32),
            pltpu.VMEM((2, NX * NC, 3, RHS, 128), F32),
            dma((10,)),
            dma((2, 9)),
            dma((2, NZ - 1)),
            dma((2, NZ)),
            dma((2,)),
            dma((2, NZ)),
            dma((2, NZ)),
            dma((2,)),
            dma((2,)),
            dma((2,)),
            dma((2,)),
        ],
        compiler_params=pltpu.CompilerParams(
            collective_id=0, has_side_effects=True, vmem_limit_bytes=60 * 1024 * 1024
        ),
    )(
        block_counts,
        near_pairs.T,
        far_group.T,
        far_local.T,
        cluster_sizes,
        right_side,
        start,
        self_blocks,
        near_blocks,
        far_factors,
    )
    return iterate, basis, norm[0, :RHS]


def solution(mesh):
    in_specs = (
        P(None, "clus"),
        P(None, "clus"),
        P("clus"),
        P(("clus", "pair"), None, None),
        P(("clus", "pair"), None, None),
        P(("clus", "pair"), None),
        P(("clus", "pair"), None, None, None),
        P(("clus", "pair"), None),
        P(("clus", "pair"), None),
        P(("clus", "pair"), None),
    )
    out_specs = (P(None, "clus"), P(None, "clus"), P())
    return jax.shard_map(local, mesh=mesh, in_specs=in_specs, out_specs=out_specs, check_vma=False)
```

```python
import functools

import jax
import jax.numpy as jnp
from jax import lax
from jax.experimental import pallas as pl
from jax.experimental.pallas import tpu as pltpu
from jax.sharding import PartitionSpec as P

PAD = 256
RHS = 8
CG = 4
RANK = 24
NZ, NX, NC, NY = 8, 4, 2, 4
GROUPS = NZ * NX * NC
PANELS = GROUPS * CG * PAD
NEAR = 16
FAR = 64
CHUNK = 16
CHUNKS = FAR // CHUNK
WIDE = CHUNK * RANK
HALF = NZ * NX * CG
PART = NX * CG
LAG = 3
UNROLL = 8

EPSILON = 1e-06
F32 = jnp.float32
BF16 = jnp.bfloat16

def fold(tile):
    return jnp.concatenate([tile[..., :128], tile[..., 128:]], axis=-2)


def unfold(tile):
    return jnp.concatenate([tile[..., :RHS, :], tile[..., RHS:, :]], axis=-1)


def dot_nt(a, b):
    return lax.dot_general(a, b, (((1,), (1,)), ((), ())), preferred_element_type=F32)


def dot_nn(a, b):
    return lax.dot_general(a, b, (((1,), (0,)), ((), ())), preferred_element_type=F32)


def ratio(a, n):
    ok = n > 1e-30
    return jnp.where(ok, a / jnp.where(ok, n, 1.0), 0.0)


def about(a, n, s, centre):
    own = ratio(a, n)
    off = own - centre
    return s + 2.0 * off * (a - own * n) + off * off * n


def kernel(
    counts_hbm,
    pairs_hbm,
    group_hbm,
    local_hbm,
    sizes_hbm,
    rhs_hbm,
    start_hbm,
    self_hbm,
    near_hbm,
    far_hbm,
    pair_ref,
    norm_ref,
    counts,
    pairs,
    groups,
    locals_,
    sizes,
    rhs_ref,
    start_ref,
    self_blk,
    near_blk,
    far_raw,
    left_all,
    right_all,
    onehot,
    row_of,
    field_first,
    field_second,
    beside_first,
    beside_second,
    own_field,
    far_back,
    near_back,
    near_in,
    spread,
    core_in,
    x_out,
    x_in,
    z_out,
    z_in,
    y_buf,
    resid,
    stats,
    load_sem,
    send_sem,
    agz_sem,
    agx_sem,
    agc_sem,
    rsc_sem,
    rsx_sem,
    rsz_sem,
    y_sem,
    beside_sem,
    near_sem,
    stat_sem,
):
    me = lax.axis_index("clus")
    y = lax.axis_index("pair")
    z, x, c = me // (NX * NC), (me // NC) % NX, me % NC

    loads = [
        pltpu.make_async_copy(src, dst, load_sem.at[i])
        for i, (src, dst) in enumerate(
            [
                (counts_hbm, counts),
                (pairs_hbm, pairs),
                (group_hbm, groups),
                (local_hbm, locals_),
                (sizes_hbm, sizes),
                (start_hbm, start_ref),
                (far_hbm, far_raw),
                (near_hbm, near_blk),
                (self_hbm, self_blk),
                (rhs_hbm, rhs_ref),
            ]
        )
    ]
    for load in loads:
        load.start()

    def dev(zz=None, xx=None, cc=None, yy=None):
        zz = z if zz is None else zz
        xx = x if xx is None else xx
        cc = c if cc is None else cc
        yy = y if yy is None else yy
        return ((zz * NX + xx) * NC + cc, yy)

    def send(src, dst, ssem, rsem, target):
        pltpu.make_async_remote_copy(
            src_ref=src,
            dst_ref=dst,
            send_sem=ssem,
            recv_sem=rsem,
            device_id=target,
            device_id_type=pl.DeviceIdType.MESH,
        ).start()

    def await_bytes(ref, sem):
        pltpu.make_async_copy(ref, ref, sem).wait()

    z_targets = [dev(zz=(z + d) % NZ) for d in range(1, NZ)]
    x_others = [(x + d) % NX for d in range(1, NX)]
    x_targets = [dev(xx=o) for o in x_others]
    y_targets = [dev(yy=(y + d) % NY) for d in range(1, NY)]
    core = dev(cc=1 - c)
    below = (me + GROUPS - 1) % GROUPS
    above = (me + 1) % GROUPS
    partners = z_targets + y_targets + x_targets + [core, (below, y), (above, y)]

    barrier = pltpu.get_barrier_semaphore()
    for target in partners:
        pl.semaphore_signal(
            barrier, inc=1, device_id=target, device_id_type=pl.DeviceIdType.MESH
        )

    for load in loads[:6]:
        load.wait()
    lane = lax.broadcasted_iota(jnp.int32, (RHS, PAD), 1)
    valid = [(lane < sizes[i]).astype(F32) for i in range(CG)]
    near_live = counts[0, 0]
    far_live = counts[0, 1]

    def base_of(group):
        return (group % NC) * HALF + (group // NC) * CG

    own_base = base_of(me)

    def far_place(k):
        group = groups[0, k]
        return (
            lax.bitwise_and(group, 1) * HALF
            + lax.shift_right_logical(group, 1) * CG
            + locals_[1, k]
        )

    diagonal = (
        lax.broadcasted_iota(jnp.int32, (CHUNK * RHS, WIDE), 0) // RHS
        == lax.broadcasted_iota(jnp.int32, (CHUNK * RHS, WIDE), 1) // RANK
    )

    def far_to_near(j):
        odd = j % 2
        return (z + NZ // 2 + (1 - 2 * odd) * ((j + 1) // 2)) % NZ

    def prepare():
        slot = lax.broadcasted_iota(jnp.int32, (RHS, WIDE), 1) // RANK

        def rows_step(chunk, carry):
            table = jnp.full((RHS, WIDE), -1, jnp.int32)
            for s in range(CHUNK):
                k = chunk * CHUNK + s
                row = jnp.where(k < far_live, locals_[0, k], -1)
                table = jnp.where(slot == s, row, table)
            row_of[chunk] = table
            return carry

        lax.fori_loop(0, CHUNKS, rows_step, 0)

        wide = lax.broadcasted_iota(jnp.int32, (RHS, FAR * RHS), 1)
        slot_of = wide // RHS

        def place_step(step, table):
            for s in range(8):
                k = step * 8 + s
                table = jnp.where(slot_of == k, far_place(k), table)
            return table

        table = lax.fori_loop(
            0, FAR // 8, place_step, jnp.full((RHS, FAR * RHS), -1, jnp.int32)
        )
        same = lax.broadcasted_iota(jnp.int32, (RHS, FAR * RHS), 0) == wide % RHS
        table = jnp.where(same, table, -1)

        def onehot_step(step, carry):
            for s in range(4):
                i = step * 4 + s
                two = jnp.concatenate(
                    [
                        jnp.where(table == 2 * i, 1.0, 0.0),
                        jnp.where(table == 2 * i + 1, 1.0, 0.0),
                    ],
                    axis=0,
                ).astype(BF16)
                onehot[pl.ds(pl.multiple_of(i * 16, 16), 16), :] = two
            return carry

        lax.fori_loop(0, GROUPS * CG // 8, onehot_step, 0)
        loads[6].wait()

        def factor_step(chunk, carry):
            rows = pl.ds(pl.multiple_of(chunk * WIDE, WIDE), WIDE)
            raw = far_raw[pl.ds(chunk * CHUNK, CHUNK)].astype(F32)
            left_all[rows, :] = raw[:, 0].reshape(WIDE, PAD).astype(BF16)
            right_all[rows, :] = raw[:, 1].reshape(WIDE, PAD).astype(BF16)
            return carry

        lax.fori_loop(0, CHUNKS, factor_step, 0)

    def apply_operator(a, values):
        field = (field_first, field_second)[a]
        beside = (beside_first, beside_second)[a]
        for i in range(CG):
            packed = values[i].astype(BF16).astype(F32)
            low = values[i] - packed if a else jnp.zeros_like(packed)
            own_field[a, i] = jnp.concatenate([packed, low], axis=0)
            field[own_base + i] = fold(packed).astype(BF16)
        mine = field.at[pl.ds(own_base, CG)]

        def send_field():
            for d, target in enumerate(z_targets):
                send(mine, mine, send_sem.at[a, 0], agz_sem.at[a, d], target)
            for target in x_targets:
                send(mine, mine, send_sem.at[a, 2], agx_sem.at[a, z], target)
            for slot, target in ((0, above), (1, below)):
                to = beside.at[pl.ds(slot * CG, CG)]
                send(mine, to, send_sem.at[a, 7], beside_sem.at[a], (target, y))

        def far_out():
            own_rows = jnp.concatenate(
                [own_field[a, i, 0:RHS] for i in range(CG)], axis=0
            ).astype(BF16)

            def back_step(chunk, carry):
                rows = pl.ds(pl.multiple_of(chunk * WIDE, WIDE), WIDE)
                every = dot_nt(own_rows, left_all[rows, :])
                table = row_of[chunk]
                coef = jnp.zeros((RHS, WIDE), F32)
                for i in range(CG):
                    coef = coef + jnp.where(
                        table == i, every[i * RHS : (i + 1) * RHS], 0.0
                    )
                tall = jnp.concatenate([coef] * CHUNK, axis=0)
                tall = jnp.where(diagonal, tall, 0.0).astype(BF16)
                out = dot_nn(tall, right_all[rows, :])
                at = pl.ds(pl.multiple_of(chunk * CHUNK * RHS, CHUNK * RHS), CHUNK * RHS)
                far_back[a, at, :] = out.astype(BF16)
                return carry

            lax.fori_loop(0, CHUNKS, back_step, 0, unroll=True)

        def near_out():
            near_back[a] = jnp.zeros((3 * CG, RHS, PAD), F32)

            def near_back_step(step, carry):
                for s in range(UNROLL):
                    k = step * UNROLL + s
                    live = jnp.where(k < near_live, 1.0, 0.0)
                    out = dot_nn(own_field[a, pairs[0, k]].astype(BF16), near_blk[k])
                    out = out[:RHS] + out[RHS:]
                    column = pairs[1, k]
                    for j in range(3 * CG):
                        near_back[a, j] += out * jnp.where(column == j, live, 0.0)
                return carry

            lax.fori_loop(0, NEAR // UNROLL, near_back_step, 0)

        def spread_part(half, zz):
            block = half * NZ + zz
            rows = pl.ds(pl.multiple_of(block * PART * RHS, PART * RHS), PART * RHS)
            out = dot_nn(onehot[rows, :], far_back[a])
            return fold(out.reshape(PART, RHS, PAD))

        def theirs_step(j, carry):
            zz = far_to_near(j)
            spread[a, zz] = spread_part(1 - c, zz).astype(BF16)
            return carry

        def to_core_step(j, carry):
            zz = far_to_near(j)
            send(
                spread.at[a, zz], core_in.at[a, zz], send_sem.at[a, 1], rsc_sem.at[a, zz], core
            )
            return carry

        def ours_step(j, carry):
            zz = far_to_near(j)
            await_bytes(core_in.at[a, zz], rsc_sem.at[a, zz])
            total = spread_part(c, zz) + core_in[a, zz].astype(F32)
            x_out[a, zz] = total.reshape(NX, CG, 16, 128).astype(BF16)
            for o in x_others:
                send(
                    x_out.at[a, zz, o],
                    x_in.at[a, zz, x],
                    send_sem.at[a, 4],
                    rsx_sem.at[a, zz],
                    dev(xx=o),
                )
            return carry

        def pass_along_x(offsets):
            for d in offsets:
                zz = (z + NZ - d) % NZ
                came = field.at[pl.ds(base_of((zz * NX + x) * NC + c), CG)]
                await_bytes(came, agz_sem.at[a, d - 1])
                for target in x_targets:
                    send(came, came, send_sem.at[a, 2], agx_sem.at[a, zz], target)

        if a == 0:
            prepare()
            far_out()
            pl.semaphore_wait(barrier, len(partners))
            send_field()
        else:
            send_field()
            far_out()

        def both(j, carry):
            return to_core_step(j, theirs_step(j, carry))

        def all_three(j, carry):
            return ours_step(j, both(j + LAG, carry))

        lax.fori_loop(0, LAG, both, 0)
        lax.fori_loop(0, NZ - LAG, all_three, 0)
        lax.fori_loop(NZ - LAG, NZ, ours_step, 0)
        if a == 0:
            loads[7].wait()
            loads[8].wait()
        else:
            share(0, [total_of([resid[i] * resid[i] for i in range(CG)])])
        pass_along_x([1, 7, 2, 6])
        near_out()
        for first, slot, target in ((0, 1, below), (2 * CG, 0, above)):
            send(
                near_back.at[a, pl.ds(first, CG)],
                near_in.at[a, slot],
                send_sem.at[a, 8],
                near_sem.at[a],
                (target, y),
            )
        pass_along_x([3, 5, 4])
        await_bytes(beside, beside_sem.at[a])

        def near_step(step, sums):
            for s in range(UNROLL):
                k = step * UNROLL + s
                column = pairs[1, k]
                inside = lax.bitwise_and(column, CG - 1)
                own = jnp.logical_and(column >= CG, column < 2 * CG)
                tile = unfold(beside[jnp.where(column < CG, 0, CG) + inside].astype(F32))
                tile = jnp.concatenate([tile, jnp.zeros_like(tile)], axis=0)
                tile = jnp.where(own, own_field[a, inside], tile).astype(BF16)
                out = dot_nt(tile, near_blk[k])
                out = out[:RHS] + out[RHS:]
                row = pairs[0, k]
                live = jnp.where(k < near_live, 1.0, 0.0)
                sums = tuple(
                    sums[i] + out * jnp.where(row == i, live, 0.0) for i in range(CG)
                )
            return sums

        sums = tuple(near_back[a, CG + i] for i in range(CG))
        sums = lax.fori_loop(0, NEAR // UNROLL, near_step, sums)

        def x_sum_step(j, carry):
            zz = far_to_near(j)
            await_bytes(x_in.at[a, zz, pl.ds(0, NX - 1)], rsx_sem.at[a, zz])
            x_in[a, zz, x] = x_out[a, zz, x]
            total = x_in[a, zz, 0].astype(F32)
            for o in range(1, NX):
                total = total + x_in[a, zz, o].astype(F32)
            z_out[a, zz] = total.astype(BF16)

            @pl.when(j < NZ - 1)
            def _():
                send(
                    z_out.at[a, zz], z_in.at[a, z], send_sem.at[a, 5], rsz_sem.at[a], dev(zz=zz)
                )

            return carry

        lax.fori_loop(0, NZ, x_sum_step, 0)

        def to_core_field(d, carry):
            zz = (z + d) % NZ
            slab = field.at[pl.ds(c * HALF + zz * PART, PART)]
            await_bytes(field.at[pl.ds(0, PART - CG)], agx_sem.at[a, zz])
            send(slab, slab, send_sem.at[a, 3], agc_sem.at[a], core)
            return carry

        lax.fori_loop(0, NZ, to_core_field, 0)

        await_bytes(field.at[pl.ds(0, HALF)], agc_sem.at[a])

        def forth_step(chunk, total):
            rows = pl.ds(pl.multiple_of(chunk * WIDE, WIDE), WIDE)
            tiles = [
                unfold(field[far_place(chunk * CHUNK + s)].astype(F32))
                for s in range(CHUNK)
            ]
            tall = jnp.concatenate(tiles, axis=0).astype(BF16)
            every = jnp.where(diagonal, dot_nt(tall, right_all[rows, :]), 0.0)
            coef = jnp.sum(every.reshape(CHUNK, RHS, WIDE), axis=0)
            table = row_of[chunk]
            four = jnp.concatenate(
                [jnp.where(table == i, coef, 0.0) for i in range(CG)], axis=0
            )
            return total + dot_nn(four.astype(BF16), left_all[rows, :])

        far_rows = lax.fori_loop(
            0, CHUNKS, forth_step, jnp.zeros((CG * RHS, PAD), F32), unroll=True
        )
        self_out = dot_nt(own_field[a, y].astype(BF16), self_blk[0])
        self_out = self_out[:RHS] + self_out[RHS:]

        await_bytes(z_in.at[a, pl.ds(0, NZ - 1)], rsz_sem.at[a])
        z_in[a, z] = z_out[a, z]
        await_bytes(near_in.at[a], near_sem.at[a])
        for i in range(CG):
            total = near_in[a, 0, i] + near_in[a, 1, i]
            total = total + sums[i] + far_rows[i * RHS : (i + 1) * RHS]
            total = total + self_out * jnp.where(y == i, 1.0, 0.0)
            come = z_in[a, 0, i].astype(F32)
            for j in range(1, NZ):
                come = come + z_in[a, j, i].astype(F32)
            y_buf[a, y, i] = total + unfold(come)
        for target in y_targets:
            send(y_buf.at[a, y], y_buf.at[a, y], send_sem.at[a, 6], y_sem.at[a], target)
        await_bytes(y_buf.at[a, pl.ds(0, NY - 1)], y_sem.at[a])
        return [
            valid[i] * (y_buf[a, 0, i] + y_buf[a, 1, i] + y_buf[a, 2, i] + y_buf[a, 3, i])
            for i in range(CG)
        ]

    sub = lax.broadcasted_iota(jnp.int32, (RHS, 128), 0)
    lane = lax.broadcasted_iota(jnp.int32, (RHS, 128), 1)

    def share(s, columns):
        spots = [
            jnp.where(lane == sub + p * RHS, column, 0.0) for p, column in enumerate(columns)
        ]
        row = functools.reduce(lambda p, q: p + q, spots)
        stats[s, pl.ds(me, 1)] = jnp.sum(row, axis=0, keepdims=True)
        part = stats.at[s, pl.ds(me, 1)]

        def step(d, carry):
            send(part, part, send_sem.at[s, 9], stat_sem.at[s], ((me + d) % GROUPS, y))
            return carry

        lax.fori_loop(1, GROUPS, step, 0)

    def shared(s):
        await_bytes(stats.at[s, pl.ds(0, GROUPS - 1)], stat_sem.at[s])
        return stats[s]

    def column_of(row):
        tall = jnp.where(lane == sub, jnp.broadcast_to(row, (RHS, 128)), 0.0)
        return jnp.sum(tall, axis=1, keepdims=True)

    def total_of(tiles):
        return jnp.sum(
            functools.reduce(lambda p, q: p + q, tiles), axis=1, keepdims=True
        )

    def cut(ref, i):
        return ref[:, i * PAD : (i + 1) * PAD]

    initial = [cut(start_ref, i) * valid[i] for i in range(CG)]
    image = apply_operator(0, initial)
    loads[9].wait()
    for i in range(CG):
        resid[i] = cut(rhs_ref, i) * valid[i] - image[i]
    image = apply_operator(1, [resid[i] for i in range(CG)])

    square = jnp.sum(shared(0), axis=0, keepdims=True)
    start_norm = jnp.sqrt(square / PANELS + EPSILON)
    norm_column = column_of(start_norm)
    basis = [resid[i] / norm_column for i in range(CG)]
    image = [image[i] / norm_column for i in range(CG)]
    inner = total_of([basis[i] * image[i] for i in range(CG)])
    size = total_of([basis[i] * basis[i] for i in range(CG)])
    centre = ratio(inner, size)
    rest = [image[i] - centre * basis[i] for i in range(CG)]
    share(1, [inner, size, total_of([rest[i] * rest[i] for i in range(CG)])])

    inner = shared(1)
    size = pltpu.roll(inner, 128 - RHS, 1)
    rest = pltpu.roll(inner, 128 - 2 * RHS, 1)
    inner_all = jnp.sum(inner, axis=0, keepdims=True)
    h_diag = inner_all / PANELS
    below_square = jnp.sum(about(inner, size, rest, h_diag), axis=0, keepdims=True)
    h_below = jnp.sqrt(jnp.maximum(below_square, 0.0) / PANELS + EPSILON)
    denominator = h_diag * h_diag + h_below * h_below
    step_size = column_of(start_norm * h_diag / denominator)
    norm_ref[...] = start_norm * h_below / jnp.sqrt(denominator)
    diag_column = column_of(h_diag)
    below_column = column_of(h_below)
    for i in range(CG):
        pair_ref[0, :, i * PAD : (i + 1) * PAD] = (
            cut(start_ref, i) * valid[i] + step_size * basis[i]
        )
        pair_ref[1, :, i * PAD : (i + 1) * PAD] = (
            image[i] - diag_column * basis[i]
        ) / below_column

    for a in range(2):
        field = (field_first, field_second)[a]
        await_bytes(field.at[pl.ds(0, CG * (NZ - 1))], send_sem.at[a, 0])
        await_bytes(spread.at[a], send_sem.at[a, 1])
        await_bytes(field.at[pl.ds(0, NZ * (NX - 1) * CG)], send_sem.at[a, 2])
        await_bytes(field.at[pl.ds(0, HALF)], send_sem.at[a, 3])
        await_bytes(x_in.at[a, pl.ds(0, NZ), pl.ds(0, NX - 1)], send_sem.at[a, 4])
        await_bytes(z_in.at[a, pl.ds(0, NZ - 1)], send_sem.at[a, 5])
        await_bytes(y_buf.at[a, pl.ds(0, NY - 1)], send_sem.at[a, 6])
        await_bytes(field.at[pl.ds(0, 2 * CG)], send_sem.at[a, 7])
        await_bytes(near_in.at[a], send_sem.at[a, 8])
        await_bytes(stats.at[a, pl.ds(0, GROUPS - 1)], send_sem.at[a, 9])


def local(
    right_side,
    start,
    cluster_sizes,
    self_blocks,
    near_blocks,
    near_pairs,
    far_factors,
    far_group,
    far_local,
    block_counts,
):
    vmem = pl.BlockSpec(memory_space=pltpu.VMEM)
    hbm = pl.BlockSpec(memory_space=pl.ANY)
    dma = pltpu.SemaphoreType.DMA
    wide = (RHS, CG * PAD)
    both, norm = pl.pallas_call(
        kernel,
        out_shape=(
            jax.ShapeDtypeStruct((2,) + wide, F32),
            jax.ShapeDtypeStruct((1, 128), F32),
        ),
        in_specs=[hbm] * 10,
        out_specs=(vmem, vmem),
        scratch_shapes=[
            pltpu.SMEM((1, 2), jnp.int32),
            pltpu.SMEM((2, NEAR), jnp.int32),
            pltpu.SMEM((1, FAR), jnp.int32),
            pltpu.SMEM((2, FAR), jnp.int32),
            pltpu.SMEM((CG,), jnp.int32),
            pltpu.VMEM(wide, F32),
            pltpu.VMEM(wide, F32),
            pltpu.VMEM((1, PAD, PAD), BF16),
            pltpu.VMEM((NEAR, PAD, PAD), BF16),
            pltpu.VMEM((FAR, 2, RANK, PAD), BF16),
            pltpu.VMEM((FAR * RANK, PAD), BF16),
            pltpu.VMEM((FAR * RANK, PAD), BF16),
            pltpu.VMEM((GROUPS * CG * RHS, FAR * RHS), BF16),
            pltpu.VMEM((CHUNKS, RHS, WIDE), jnp.int32),
            pltpu.VMEM((GROUPS * CG, 16, 128), BF16),
            pltpu.VMEM((GROUPS * CG, 16, 128), BF16),
            pltpu.VMEM((2 * CG, 16, 128), BF16),
            pltpu.VMEM((2 * CG, 16, 128), BF16),
            pltpu.VMEM((2, CG, 2 * RHS, PAD), F32),
            pltpu.VMEM((2, FAR * RHS, PAD), BF16),
            pltpu.VMEM((2, 3 * CG, RHS, PAD), F32),
            pltpu.VMEM((2, 2, CG, RHS, PAD), F32),
            pltpu.VMEM((2, NZ, PART, 16, 128), BF16),
            pltpu.VMEM((2, NZ, PART, 16, 128), BF16),
            pltpu.VMEM((2, NZ, NX, CG, 16, 128), BF16),
            pltpu.VMEM((2, NZ, NX, CG, 16, 128), BF16),
            pltpu.VMEM((2, NZ, CG, 16, 128), BF16),
            pltpu.VMEM((2, NZ, CG, 16, 128), BF16),
            pltpu.VMEM((2, NY, CG, RHS, PAD), F32),
            pltpu.VMEM((CG, RHS, PAD), F32),
            pltpu.VMEM((2, GROUPS, 128), F32),
            dma((10,)),
            dma((2, 10)),
            dma((2, NZ - 1)),
            dma((2, NZ)),
            dma((2,)),
            dma((2, NZ)),
            dma((2, NZ)),
            dma((2,)),
            dma((2,)),
            dma((2,)),
            dma((2,)),
            dma((2,)),
        ],
        compiler_params=pltpu.CompilerParams(
            collective_id=0, has_side_effects=True, vmem_limit_bytes=60 * 1024 * 1024
        ),
    )(
        block_counts,
        near_pairs.T,
        far_group.T,
        far_local.T,
        cluster_sizes,
        right_side,
        start,
        self_blocks,
        near_blocks,
        far_factors,
    )
    return both[0], both[1], norm[0, :RHS]


def solution(mesh):
    in_specs = (
        P(None, "clus"),
        P(None, "clus"),
        P("clus"),
        P(("clus", "pair"), None, None),
        P(("clus", "pair"), None, None),
        P(("clus", "pair"), None),
        P(("clus", "pair"), None, None, None),
        P(("clus", "pair"), None),
        P(("clus", "pair"), None),
        P(("clus", "pair"), None),
    )
    out_specs = (P(None, "clus"), P(None, "clus"), P())
    return jax.shard_map(local, mesh=mesh, in_specs=in_specs, out_specs=out_specs, check_vma=False)
```

```python
import functools

import jax
import jax.numpy as jnp
from jax import lax
from jax.experimental import pallas as pl
from jax.experimental.pallas import tpu as pltpu
from jax.sharding import PartitionSpec as P

PAD = 256
RHS = 8
CG = 4
RANK = 24
NZ, NX, NC, NY = 8, 4, 2, 4
GROUPS = NZ * NX * NC
PANELS = GROUPS * CG * PAD
NEAR = 16
FAR = 64
CHUNK = 16
CHUNKS = FAR // CHUNK
WIDE = CHUNK * RANK
HALF = NZ * NX * CG
PART = NX * CG
LAG = 3
UNROLL = 8

EPSILON = 1e-06
F32 = jnp.float32
BF16 = jnp.bfloat16

def fold(tile):
    return jnp.concatenate([tile[..., :128], tile[..., 128:]], axis=-2)


def unfold(tile):
    return jnp.concatenate([tile[..., :RHS, :], tile[..., RHS:, :]], axis=-1)


def dot_nt(a, b):
    return lax.dot_general(a, b, (((1,), (1,)), ((), ())), preferred_element_type=F32)


def dot_nn(a, b):
    return lax.dot_general(a, b, (((1,), (0,)), ((), ())), preferred_element_type=F32)


def ratio(a, n):
    ok = n > 1e-30
    return jnp.where(ok, a / jnp.where(ok, n, 1.0), 0.0)


def about(a, n, s, centre):
    own = ratio(a, n)
    off = own - centre
    return s + 2.0 * off * (a - own * n) + off * off * n


def kernel(
    counts_hbm,
    pairs_hbm,
    group_hbm,
    local_hbm,
    sizes_hbm,
    rhs_hbm,
    start_hbm,
    self_hbm,
    near_hbm,
    far_hbm,
    pair_ref,
    norm_ref,
    counts,
    pairs,
    groups,
    locals_,
    sizes,
    rhs_ref,
    start_ref,
    self_blk,
    near_blk,
    far_raw,
    left_all,
    right_all,
    onehot,
    row_of,
    field_first,
    field_second,
    beside_first,
    beside_second,
    own_field,
    own_tiles,
    far_back,
    near_back,
    near_in,
    spread,
    core_in,
    x_out,
    x_in,
    z_out,
    z_in,
    y_buf,
    resid,
    stats,
    load_sem,
    send_sem,
    agz_sem,
    agx_sem,
    agy_sem,
    agc_sem,
    rsc_sem,
    rsx_sem,
    rsz_sem,
    y_sem,
    beside_sem,
    near_sem,
    stat_sem,
):
    me = lax.axis_index("clus")
    y = lax.axis_index("pair")
    z, x, c = me // (NX * NC), (me // NC) % NX, me % NC

    loads = [
        pltpu.make_async_copy(src, dst, load_sem.at[i])
        for i, (src, dst) in enumerate(
            [
                (counts_hbm, counts),
                (pairs_hbm, pairs),
                (group_hbm, groups),
                (local_hbm, locals_),
                (sizes_hbm, sizes),
                (start_hbm, start_ref),
                (far_hbm, far_raw),
                (near_hbm, near_blk),
                (self_hbm, self_blk),
                (rhs_hbm, rhs_ref),
            ]
        )
    ]
    for load in loads:
        load.start()

    def dev(zz=None, xx=None, cc=None, yy=None):
        zz = z if zz is None else zz
        xx = x if xx is None else xx
        cc = c if cc is None else cc
        yy = y if yy is None else yy
        return ((zz * NX + xx) * NC + cc, yy)

    def send(src, dst, ssem, rsem, target):
        pltpu.make_async_remote_copy(
            src_ref=src,
            dst_ref=dst,
            send_sem=ssem,
            recv_sem=rsem,
            device_id=target,
            device_id_type=pl.DeviceIdType.MESH,
        ).start()

    def await_bytes(ref, sem):
        pltpu.make_async_copy(ref, ref, sem).wait()

    z_targets = [dev(zz=(z + d) % NZ) for d in range(1, NZ)]
    x_others = [(x + d) % NX for d in range(1, NX)]
    x_targets = [dev(xx=o) for o in x_others]
    y_targets = [dev(yy=(y + d) % NY) for d in range(1, NY)]
    core = dev(cc=1 - c)
    below = (me + GROUPS - 1) % GROUPS
    above = (me + 1) % GROUPS
    zx_targets = [
        dev(zz=(z + dz) % NZ, xx=(x + dx) % NX)
        for dz in (4, 3, 5, 2, 6, 1, 7, 0)
        for dx in (2, 1, 3, 0)
        if dz or dx
    ]
    partners = zx_targets + y_targets + [core, (below, y), (above, y)]

    barrier = pltpu.get_barrier_semaphore()
    for target in partners:
        pl.semaphore_signal(
            barrier, inc=1, device_id=target, device_id_type=pl.DeviceIdType.MESH
        )

    for load in loads[:6]:
        load.wait()
    lane = lax.broadcasted_iota(jnp.int32, (RHS, PAD), 1)
    valid = [(lane < sizes[i]).astype(F32) for i in range(CG)]
    near_live = counts[0, 0]
    far_live = counts[0, 1]


    def far_place(k):
        group = groups[0, k]
        return (
            lax.bitwise_and(group, 1) * HALF
            + lax.shift_right_logical(group, 1) * CG
            + locals_[1, k]
        )

    def far_tile(k):
        group = groups[0, k]
        return (
            lax.bitwise_and(group, 1) * HALF
            + lax.shift_right_logical(group, 3) * PART
            + locals_[1, k] * NX
            + lax.bitwise_and(lax.shift_right_logical(group, 1), NX - 1)
        )

    def field_at(zz, cluster, xx):
        return c * HALF + zz * PART + cluster * NX + xx

    diagonal = (
        lax.broadcasted_iota(jnp.int32, (CHUNK * RHS, WIDE), 0) // RHS
        == lax.broadcasted_iota(jnp.int32, (CHUNK * RHS, WIDE), 1) // RANK
    )

    def far_to_near(j):
        odd = j % 2
        return (z + NZ // 2 + (1 - 2 * odd) * ((j + 1) // 2)) % NZ

    def prepare():
        slot = lax.broadcasted_iota(jnp.int32, (RHS, WIDE), 1) // RANK

        def rows_step(chunk, carry):
            table = jnp.full((RHS, WIDE), -1, jnp.int32)
            for s in range(CHUNK):
                k = chunk * CHUNK + s
                row = jnp.where(k < far_live, locals_[0, k], -1)
                table = jnp.where(slot == s, row, table)
            row_of[chunk] = table
            return carry

        lax.fori_loop(0, CHUNKS, rows_step, 0)

        wide = lax.broadcasted_iota(jnp.int32, (RHS, FAR * RHS), 1)
        slot_of = wide // RHS

        def place_step(step, table):
            for s in range(8):
                k = step * 8 + s
                table = jnp.where(slot_of == k, far_place(k), table)
            return table

        table = lax.fori_loop(
            0, FAR // 8, place_step, jnp.full((RHS, FAR * RHS), -1, jnp.int32)
        )
        same = lax.broadcasted_iota(jnp.int32, (RHS, FAR * RHS), 0) == wide % RHS
        table = jnp.where(same, table, -1)

        def onehot_step(step, carry):
            for s in range(4):
                i = step * 4 + s
                two = jnp.concatenate(
                    [
                        jnp.where(table == 2 * i, 1.0, 0.0),
                        jnp.where(table == 2 * i + 1, 1.0, 0.0),
                    ],
                    axis=0,
                ).astype(BF16)
                onehot[pl.ds(pl.multiple_of(i * 16, 16), 16), :] = two
            return carry

        lax.fori_loop(0, GROUPS * CG // 8, onehot_step, 0)
        loads[6].wait()

        def factor_step(chunk, carry):
            rows = pl.ds(pl.multiple_of(chunk * WIDE, WIDE), WIDE)
            raw = far_raw[pl.ds(chunk * CHUNK, CHUNK)].astype(F32)
            left_all[rows, :] = raw[:, 0].reshape(WIDE, PAD).astype(BF16)
            right_all[rows, :] = raw[:, 1].reshape(WIDE, PAD).astype(BF16)
            return carry

        lax.fori_loop(0, CHUNKS, factor_step, 0)

    def apply_operator(a, values):
        field = (field_first, field_second)[a]
        beside = (beside_first, beside_second)[a]
        for i in range(CG):
            packed = values[i].astype(BF16).astype(F32)
            low = values[i] - packed if a else jnp.zeros_like(packed)
            own_field[a, i] = jnp.concatenate([packed, low], axis=0)
            own_tiles[a, i] = fold(packed).astype(BF16)

        def send_field():
            own = own_tiles.at[a, y]
            here = field.at[field_at(z, y, x)]
            for to in zx_targets:
                send(own, here, send_sem.at[a, 2], agx_sem.at[a, z], to)
            for slot, target in ((0, above), (1, below)):
                to = beside.at[pl.ds(slot * CG, CG)]
                send(own_tiles.at[a], to, send_sem.at[a, 7], beside_sem.at[a], (target, y))
            field[field_at(z, y, x)] = own_tiles[a, y]

        def far_out():
            own_rows = jnp.concatenate(
                [own_field[a, i, 0:RHS] for i in range(CG)], axis=0
            ).astype(BF16)

            def back_step(chunk, carry):
                rows = pl.ds(pl.multiple_of(chunk * WIDE, WIDE), WIDE)
                every = dot_nt(own_rows, left_all[rows, :])
                table = row_of[chunk]
                coef = jnp.zeros((RHS, WIDE), F32)
                for i in range(CG):
                    coef = coef + jnp.where(
                        table == i, every[i * RHS : (i + 1) * RHS], 0.0
                    )
                tall = jnp.concatenate([coef] * CHUNK, axis=0)
                tall = jnp.where(diagonal, tall, 0.0).astype(BF16)
                out = dot_nn(tall, right_all[rows, :])
                at = pl.ds(pl.multiple_of(chunk * CHUNK * RHS, CHUNK * RHS), CHUNK * RHS)
                far_back[a, at, :] = out.astype(BF16)
                return carry

            lax.fori_loop(0, CHUNKS, back_step, 0, unroll=True)

        def near_out():
            near_back[a] = jnp.zeros((3 * CG, RHS, PAD), F32)

            def near_back_step(step, carry):
                for s in range(UNROLL):
                    k = step * UNROLL + s
                    live = jnp.where(k < near_live, 1.0, 0.0)
                    out = dot_nn(own_field[a, pairs[0, k]].astype(BF16), near_blk[k])
                    out = out[:RHS] + out[RHS:]
                    column = pairs[1, k]
                    for j in range(3 * CG):
                        near_back[a, j] += out * jnp.where(column == j, live, 0.0)
                return carry

            lax.fori_loop(0, NEAR // UNROLL, near_back_step, 0)

        def spread_part(half, zz):
            block = half * NZ + zz
            rows = pl.ds(pl.multiple_of(block * PART * RHS, PART * RHS), PART * RHS)
            out = dot_nn(onehot[rows, :], far_back[a])
            return fold(out.reshape(PART, RHS, PAD))

        def theirs_step(j, carry):
            zz = far_to_near(j)
            spread[a, zz] = spread_part(1 - c, zz).astype(BF16)
            return carry

        def to_core_step(j, carry):
            zz = far_to_near(j)
            send(
                spread.at[a, zz], core_in.at[a, zz], send_sem.at[a, 1], rsc_sem.at[a, zz], core
            )
            return carry

        def ours_step(j, carry):
            zz = far_to_near(j)
            await_bytes(core_in.at[a, zz], rsc_sem.at[a, zz])
            total = spread_part(c, zz) + core_in[a, zz].astype(F32)
            x_out[a, zz] = total.reshape(NX, CG, 16, 128).astype(BF16)
            for o in x_others:
                send(
                    x_out.at[a, zz, o],
                    x_in.at[a, zz, x],
                    send_sem.at[a, 4],
                    rsx_sem.at[a, zz],
                    dev(xx=o),
                )
            return carry

        def along_y(d):
            zz = (z + NZ - d) % NZ
            run = field.at[pl.ds(field_at(zz, y, 0), NX)]
            await_bytes(field.at[pl.ds(0, NX if d else NX - 1)], agx_sem.at[a, zz])
            for target in y_targets:
                send(run, run, send_sem.at[a, 10], agy_sem.at[a, zz], target)

        def to_other_core(d):
            zz = (z + NZ - d) % NZ
            slab = field.at[pl.ds(field_at(zz, 0, 0), PART)]
            await_bytes(field.at[pl.ds(0, PART - NX)], agy_sem.at[a, zz])
            send(slab, slab, send_sem.at[a, 3], agc_sem.at[a], core)

        if a == 0:
            prepare()
            far_out()
            lax.fori_loop(0, NZ, theirs_step, 0)
            pl.semaphore_wait(barrier, len(partners))
            send_field()
            lax.fori_loop(0, NZ, to_core_step, 0)
            lax.fori_loop(0, NZ, ours_step, 0)
        else:
            send_field()
            far_out()

            def both(j, carry):
                return to_core_step(j, theirs_step(j, carry))

            def all_three(j, carry):
                return ours_step(j, both(j + LAG, carry))

            lax.fori_loop(0, LAG, both, 0)
            lax.fori_loop(0, NZ - LAG, all_three, 0)
            lax.fori_loop(NZ - LAG, NZ, ours_step, 0)
        if a == 0:
            loads[7].wait()
            loads[8].wait()
        order = [0, 1, 7, 2, 6, 3, 5, 4]
        along_y(0)
        along_y(1)
        along_y(7)
        near_out()
        for first, slot, target in ((0, 1, below), (2 * CG, 0, above)):
            send(
                near_back.at[a, pl.ds(first, CG)],
                near_in.at[a, slot],
                send_sem.at[a, 8],
                near_sem.at[a],
                (target, y),
            )
        along_y(2)
        along_y(6)
        await_bytes(beside, beside_sem.at[a])

        def near_step(step, sums):
            for s in range(UNROLL):
                k = step * UNROLL + s
                column = pairs[1, k]
                inside = lax.bitwise_and(column, CG - 1)
                own = jnp.logical_and(column >= CG, column < 2 * CG)
                tile = unfold(beside[jnp.where(column < CG, 0, CG) + inside].astype(F32))
                tile = jnp.concatenate([tile, jnp.zeros_like(tile)], axis=0)
                tile = jnp.where(own, own_field[a, inside], tile).astype(BF16)
                out = dot_nt(tile, near_blk[k])
                out = out[:RHS] + out[RHS:]
                row = pairs[0, k]
                live = jnp.where(k < near_live, 1.0, 0.0)
                sums = tuple(
                    sums[i] + out * jnp.where(row == i, live, 0.0) for i in range(CG)
                )
            return sums

        sums = tuple(near_back[a, CG + i] for i in range(CG))
        sums = lax.fori_loop(0, NEAR // UNROLL, near_step, sums)
        along_y(3)
        along_y(5)
        along_y(4)

        def x_sum_step(j):
            zz = far_to_near(j)
            await_bytes(x_in.at[a, zz, pl.ds(0, NX - 1)], rsx_sem.at[a, zz])
            x_in[a, zz, x] = x_out[a, zz, x]
            total = x_in[a, zz, 0].astype(F32)
            for o in range(1, NX):
                total = total + x_in[a, zz, o].astype(F32)
            z_out[a, zz] = total.astype(BF16)
            if j < NZ - 1:
                send(
                    z_out.at[a, zz], z_in.at[a, z], send_sem.at[a, 5], rsz_sem.at[a], dev(zz=zz)
                )

        for j in range(NZ):
            x_sum_step(j)
        for j in range(NZ):
            to_other_core(order[j])
        if a:
            share(0, [total_of([resid[i] * resid[i] for i in range(CG)])])

        await_bytes(field.at[pl.ds(0, HALF)], agc_sem.at[a])

        def forth_step(chunk, total):
            rows = pl.ds(pl.multiple_of(chunk * WIDE, WIDE), WIDE)
            tiles = [
                unfold(field[far_tile(chunk * CHUNK + s)].astype(F32))
                for s in range(CHUNK)
            ]
            tall = jnp.concatenate(tiles, axis=0).astype(BF16)
            every = jnp.where(diagonal, dot_nt(tall, right_all[rows, :]), 0.0)
            coef = jnp.sum(every.reshape(CHUNK, RHS, WIDE), axis=0)
            table = row_of[chunk]
            four = jnp.concatenate(
                [jnp.where(table == i, coef, 0.0) for i in range(CG)], axis=0
            )
            return total + dot_nn(four.astype(BF16), left_all[rows, :])

        far_rows = lax.fori_loop(
            0, CHUNKS, forth_step, jnp.zeros((CG * RHS, PAD), F32), unroll=True
        )
        self_out = dot_nt(own_field[a, y].astype(BF16), self_blk[0])
        self_out = self_out[:RHS] + self_out[RHS:]

        await_bytes(z_in.at[a, pl.ds(0, NZ - 1)], rsz_sem.at[a])
        z_in[a, z] = z_out[a, z]
        await_bytes(near_in.at[a], near_sem.at[a])
        for i in range(CG):
            total = near_in[a, 0, i] + near_in[a, 1, i]
            total = total + sums[i] + far_rows[i * RHS : (i + 1) * RHS]
            total = total + self_out * jnp.where(y == i, 1.0, 0.0)
            come = z_in[a, 0, i].astype(F32)
            for j in range(1, NZ):
                come = come + z_in[a, j, i].astype(F32)
            y_buf[a, y, i] = total + unfold(come)
        for target in y_targets:
            send(y_buf.at[a, y], y_buf.at[a, y], send_sem.at[a, 6], y_sem.at[a], target)
        await_bytes(y_buf.at[a, pl.ds(0, NY - 1)], y_sem.at[a])
        return [
            valid[i] * (y_buf[a, 0, i] + y_buf[a, 1, i] + y_buf[a, 2, i] + y_buf[a, 3, i])
            for i in range(CG)
        ]

    sub = lax.broadcasted_iota(jnp.int32, (RHS, 128), 0)
    lane = lax.broadcasted_iota(jnp.int32, (RHS, 128), 1)

    def share(s, columns):
        spots = [
            jnp.where(lane == sub + p * RHS, column, 0.0) for p, column in enumerate(columns)
        ]
        row = functools.reduce(lambda p, q: p + q, spots)
        stats[s, pl.ds(me, 1)] = jnp.sum(row, axis=0, keepdims=True)
        part = stats.at[s, pl.ds(me, 1)]

        def step(d, carry):
            send(part, part, send_sem.at[s, 9], stat_sem.at[s], ((me + d) % GROUPS, y))
            return carry

        lax.fori_loop(1, GROUPS, step, 0)

    def shared(s):
        await_bytes(stats.at[s, pl.ds(0, GROUPS - 1)], stat_sem.at[s])
        return stats[s]

    def column_of(row):
        tall = jnp.where(lane == sub, jnp.broadcast_to(row, (RHS, 128)), 0.0)
        return jnp.sum(tall, axis=1, keepdims=True)

    def total_of(tiles):
        return jnp.sum(
            functools.reduce(lambda p, q: p + q, tiles), axis=1, keepdims=True
        )

    def cut(ref, i):
        return ref[:, i * PAD : (i + 1) * PAD]

    initial = [cut(start_ref, i) * valid[i] for i in range(CG)]
    image = apply_operator(0, initial)
    loads[9].wait()
    for i in range(CG):
        resid[i] = cut(rhs_ref, i) * valid[i] - image[i]
    image = apply_operator(1, [resid[i] for i in range(CG)])

    square = jnp.sum(shared(0), axis=0, keepdims=True)
    start_norm = jnp.sqrt(square / PANELS + EPSILON)
    norm_column = column_of(start_norm)
    basis = [resid[i] / norm_column for i in range(CG)]
    image = [image[i] / norm_column for i in range(CG)]
    inner = total_of([basis[i] * image[i] for i in range(CG)])
    size = total_of([basis[i] * basis[i] for i in range(CG)])
    centre = ratio(inner, size)
    rest = [image[i] - centre * basis[i] for i in range(CG)]
    share(1, [inner, size, total_of([rest[i] * rest[i] for i in range(CG)])])

    inner = shared(1)
    size = pltpu.roll(inner, 128 - RHS, 1)
    rest = pltpu.roll(inner, 128 - 2 * RHS, 1)
    inner_all = jnp.sum(inner, axis=0, keepdims=True)
    h_diag = inner_all / PANELS
    below_square = jnp.sum(about(inner, size, rest, h_diag), axis=0, keepdims=True)
    h_below = jnp.sqrt(jnp.maximum(below_square, 0.0) / PANELS + EPSILON)
    denominator = h_diag * h_diag + h_below * h_below
    step_size = column_of(start_norm * h_diag / denominator)
    norm_ref[...] = start_norm * h_below / jnp.sqrt(denominator)
    diag_column = column_of(h_diag)
    below_column = column_of(h_below)
    for i in range(CG):
        pair_ref[0, :, i * PAD : (i + 1) * PAD] = (
            cut(start_ref, i) * valid[i] + step_size * basis[i]
        )
        pair_ref[1, :, i * PAD : (i + 1) * PAD] = (
            image[i] - diag_column * basis[i]
        ) / below_column

    for a in range(2):
        field = (field_first, field_second)[a]
        await_bytes(spread.at[a], send_sem.at[a, 1])
        await_bytes(field.at[pl.ds(0, NZ * NX - 1)], send_sem.at[a, 2])
        await_bytes(field.at[pl.ds(0, NZ * (NY - 1) * NX)], send_sem.at[a, 10])
        await_bytes(field.at[pl.ds(0, HALF)], send_sem.at[a, 3])
        await_bytes(x_in.at[a, pl.ds(0, NZ), pl.ds(0, NX - 1)], send_sem.at[a, 4])
        await_bytes(z_in.at[a, pl.ds(0, NZ - 1)], send_sem.at[a, 5])
        await_bytes(y_buf.at[a, pl.ds(0, NY - 1)], send_sem.at[a, 6])
        await_bytes(field.at[pl.ds(0, 2 * CG)], send_sem.at[a, 7])
        await_bytes(near_in.at[a], send_sem.at[a, 8])
        await_bytes(stats.at[a, pl.ds(0, GROUPS - 1)], send_sem.at[a, 9])


def local(
    right_side,
    start,
    cluster_sizes,
    self_blocks,
    near_blocks,
    near_pairs,
    far_factors,
    far_group,
    far_local,
    block_counts,
):
    vmem = pl.BlockSpec(memory_space=pltpu.VMEM)
    hbm = pl.BlockSpec(memory_space=pl.ANY)
    dma = pltpu.SemaphoreType.DMA
    wide = (RHS, CG * PAD)
    both, norm = pl.pallas_call(
        kernel,
        out_shape=(
            jax.ShapeDtypeStruct((2,) + wide, F32),
            jax.ShapeDtypeStruct((1, 128), F32),
        ),
        in_specs=[hbm] * 10,
        out_specs=(vmem, vmem),
        scratch_shapes=[
            pltpu.SMEM((1, 2), jnp.int32),
            pltpu.SMEM((2, NEAR), jnp.int32),
            pltpu.SMEM((1, FAR), jnp.int32),
            pltpu.SMEM((2, FAR), jnp.int32),
            pltpu.SMEM((CG,), jnp.int32),
            pltpu.VMEM(wide, F32),
            pltpu.VMEM(wide, F32),
            pltpu.VMEM((1, PAD, PAD), BF16),
            pltpu.VMEM((NEAR, PAD, PAD), BF16),
            pltpu.VMEM((FAR, 2, RANK, PAD), BF16),
            pltpu.VMEM((FAR * RANK, PAD), BF16),
            pltpu.VMEM((FAR * RANK, PAD), BF16),
            pltpu.VMEM((GROUPS * CG * RHS, FAR * RHS), BF16),
            pltpu.VMEM((CHUNKS, RHS, WIDE), jnp.int32),
            pltpu.VMEM((GROUPS * CG, 16, 128), BF16),
            pltpu.VMEM((GROUPS * CG, 16, 128), BF16),
            pltpu.VMEM((2 * CG, 16, 128), BF16),
            pltpu.VMEM((2 * CG, 16, 128), BF16),
            pltpu.VMEM((2, CG, 2 * RHS, PAD), F32),
            pltpu.VMEM((2, CG, 16, 128), BF16),
            pltpu.VMEM((2, FAR * RHS, PAD), BF16),
            pltpu.VMEM((2, 3 * CG, RHS, PAD), F32),
            pltpu.VMEM((2, 2, CG, RHS, PAD), F32),
            pltpu.VMEM((2, NZ, PART, 16, 128), BF16),
            pltpu.VMEM((2, NZ, PART, 16, 128), BF16),
            pltpu.VMEM((2, NZ, NX, CG, 16, 128), BF16),
            pltpu.VMEM((2, NZ, NX, CG, 16, 128), BF16),
            pltpu.VMEM((2, NZ, CG, 16, 128), BF16),
            pltpu.VMEM((2, NZ, CG, 16, 128), BF16),
            pltpu.VMEM((2, NY, CG, RHS, PAD), F32),
            pltpu.VMEM((CG, RHS, PAD), F32),
            pltpu.VMEM((2, GROUPS, 128), F32),
            dma((10,)),
            dma((2, 11)),
            dma((2, NZ - 1)),
            dma((2, NZ)),
            dma((2, NZ)),
            dma((2,)),
            dma((2, NZ)),
            dma((2, NZ)),
            dma((2,)),
            dma((2,)),
            dma((2,)),
            dma((2,)),
            dma((2,)),
        ],
        compiler_params=pltpu.CompilerParams(
            collective_id=0, has_side_effects=True, vmem_limit_bytes=60 * 1024 * 1024
        ),
    )(
        block_counts,
        near_pairs.T,
        far_group.T,
        far_local.T,
        cluster_sizes,
        right_side,
        start,
        self_blocks,
        near_blocks,
        far_factors,
    )
    return both[0], both[1], norm[0, :RHS]


def solution(mesh):
    in_specs = (
        P(None, "clus"),
        P(None, "clus"),
        P("clus"),
        P(("clus", "pair"), None, None),
        P(("clus", "pair"), None, None),
        P(("clus", "pair"), None),
        P(("clus", "pair"), None, None, None),
        P(("clus", "pair"), None),
        P(("clus", "pair"), None),
        P(("clus", "pair"), None),
    )
    out_specs = (P(None, "clus"), P(None, "clus"), P())
    return jax.shard_map(local, mesh=mesh, in_specs=in_specs, out_specs=out_specs, check_vma=False)
```

```python
import functools

import jax
import jax.numpy as jnp
from jax import lax
from jax.experimental import pallas as pl
from jax.experimental.pallas import tpu as pltpu
from jax.sharding import PartitionSpec as P

PAD = 256
RHS = 8
CG = 4
RANK = 24
NZ, NX, NC, NY = 8, 4, 2, 4
GROUPS = NZ * NX * NC
PANELS = GROUPS * CG * PAD
NEAR = 16
FAR = 64
CHUNK = 16
CHUNKS = FAR // CHUNK
WIDE = CHUNK * RANK
HALF = NZ * NX * CG
PART = NX * CG
NEAR_Z = (0,)
LAG = 3
UNROLL = 8

EPSILON = 1e-06
F32 = jnp.float32
BF16 = jnp.bfloat16

def fold(tile):
    return jnp.concatenate([tile[..., :128], tile[..., 128:]], axis=-2)


def unfold(tile):
    return jnp.concatenate([tile[..., :RHS, :], tile[..., RHS:, :]], axis=-1)


def dot_nt(a, b):
    return lax.dot_general(a, b, (((1,), (1,)), ((), ())), preferred_element_type=F32)


def dot_nn(a, b):
    return lax.dot_general(a, b, (((1,), (0,)), ((), ())), preferred_element_type=F32)


def ratio(a, n):
    ok = n > 1e-30
    return jnp.where(ok, a / jnp.where(ok, n, 1.0), 0.0)


def about(a, n, s, centre):
    own = ratio(a, n)
    off = own - centre
    return s + 2.0 * off * (a - own * n) + off * off * n


def kernel(
    counts_hbm,
    pairs_hbm,
    group_hbm,
    local_hbm,
    sizes_hbm,
    rhs_hbm,
    start_hbm,
    self_hbm,
    near_hbm,
    far_hbm,
    pair_ref,
    norm_ref,
    counts,
    pairs,
    groups,
    locals_,
    sizes,
    rhs_ref,
    start_ref,
    self_blk,
    near_blk,
    far_raw,
    left_all,
    right_all,
    onehot,
    row_of,
    field_first,
    field_second,
    beside_first,
    beside_second,
    own_field,
    own_tiles,
    far_back,
    near_back,
    near_in,
    spread,
    core_in,
    x_out,
    x_in,
    z_out,
    z_in,
    y_buf,
    resid,
    stats,
    load_sem,
    send_sem,
    agz_sem,
    agx_sem,
    agy_sem,
    agc_sem,
    rsc_sem,
    rsx_sem,
    rsz_sem,
    y_sem,
    beside_sem,
    near_sem,
    stat_sem,
):
    me = lax.axis_index("clus")
    y = lax.axis_index("pair")
    z = lax.shift_right_logical(me, 3)
    x = lax.bitwise_and(lax.shift_right_logical(me, 1), NX - 1)
    c = lax.bitwise_and(me, NC - 1)

    loads = [
        pltpu.make_async_copy(src, dst, load_sem.at[i])
        for i, (src, dst) in enumerate(
            [
                (counts_hbm, counts),
                (pairs_hbm, pairs),
                (group_hbm, groups),
                (local_hbm, locals_),
                (sizes_hbm, sizes),
                (start_hbm, start_ref),
                (far_hbm, far_raw),
                (near_hbm, near_blk),
                (self_hbm, self_blk),
                (rhs_hbm, rhs_ref),
            ]
        )
    ]
    for load in loads:
        load.start()

    def wrap(value, size):
        return lax.bitwise_and(value, size - 1)

    def dev(zz=None, xx=None, cc=None, yy=None):
        zz = z if zz is None else zz
        xx = x if xx is None else xx
        cc = c if cc is None else cc
        yy = y if yy is None else yy
        return ((zz * NX + xx) * NC + cc, yy)

    def send(src, dst, ssem, rsem, target):
        pltpu.make_async_remote_copy(
            src_ref=src,
            dst_ref=dst,
            send_sem=ssem,
            recv_sem=rsem,
            device_id=target,
            device_id_type=pl.DeviceIdType.MESH,
        ).start()

    def await_bytes(ref, sem):
        pltpu.make_async_copy(ref, ref, sem).wait()

    x_others = [wrap(x + d, NX) for d in range(1, NX)]
    x_targets = [dev(xx=o) for o in x_others]
    y_targets = [dev(yy=wrap(y + d, NY)) for d in range(1, NY)]
    core = dev(cc=1 - c)
    below = wrap(me + GROUPS - 1, GROUPS)
    above = wrap(me + 1, GROUPS)
    def hops(place):
        dz, dx, dc = place
        return min(dz, NZ - dz) + min(dx, NX - dx) + 0.5 * dc

    places = [(i, j, k) for i in range(NZ) for j in range(NX) for k in range(NC)]
    everyone = [
        dev(zz=wrap(z + i, NZ), xx=wrap(x + j, NX), cc=wrap(c + k, NC))
        for i, j, k in sorted(places, key=hops, reverse=True)
        if i or j or k
    ]
    zx_targets = [
        (dz, dev(zz=wrap(z + dz, NZ), xx=wrap(x + dx, NX)))
        for dz in (4, 3, 5, 2, 6, 1, 7, 0)
        for dx in (2, 1, 3, 0)
        if dz or dx
    ]
    partners = [target for _, target in zx_targets] + y_targets + [core, (below, y), (above, y)]

    barrier = pltpu.get_barrier_semaphore()
    for target in partners:
        pl.semaphore_signal(
            barrier, inc=1, device_id=target, device_id_type=pl.DeviceIdType.MESH
        )

    for load in loads[:6]:
        load.wait()
    lane = lax.broadcasted_iota(jnp.int32, (RHS, PAD), 1)
    valid = [(lane < sizes[i]).astype(F32) for i in range(CG)]
    near_live = counts[0, 0]
    far_live = counts[0, 1]


    def far_place(k):
        group = groups[0, k]
        return (
            lax.bitwise_and(group, 1) * HALF
            + lax.shift_right_logical(group, 1) * CG
            + locals_[1, k]
        )

    def far_tile(k):
        group = groups[0, k]
        return (
            lax.bitwise_and(group, 1) * NZ + lax.shift_right_logical(group, 3),
            locals_[1, k],
            lax.bitwise_and(lax.shift_right_logical(group, 1), NX - 1),
        )

    diagonal = (
        lax.broadcasted_iota(jnp.int32, (CHUNK * RHS, WIDE), 0) // RHS
        == lax.broadcasted_iota(jnp.int32, (CHUNK * RHS, WIDE), 1) // RANK
    )

    def far_to_near(j):
        odd = j % 2
        return wrap(z + NZ // 2 + (1 - 2 * odd) * ((j + 1) // 2), NZ)

    def prepare():
        slot = lax.broadcasted_iota(jnp.int32, (RHS, WIDE), 1) // RANK

        def rows_step(chunk, carry):
            table = jnp.full((RHS, WIDE), -1, jnp.int32)
            for s in range(CHUNK):
                k = chunk * CHUNK + s
                row = jnp.where(k < far_live, locals_[0, k], -1)
                table = jnp.where(slot == s, row, table)
            row_of[chunk] = table
            return carry

        lax.fori_loop(0, CHUNKS, rows_step, 0)

        wide = lax.broadcasted_iota(jnp.int32, (RHS, FAR * RHS), 1)
        slot_of = wide // RHS

        def place_step(step, table):
            for s in range(8):
                k = step * 8 + s
                table = jnp.where(slot_of == k, far_place(k), table)
            return table

        table = lax.fori_loop(
            0, FAR // 8, place_step, jnp.full((RHS, FAR * RHS), -1, jnp.int32)
        )
        same = lax.broadcasted_iota(jnp.int32, (RHS, FAR * RHS), 0) == wide % RHS
        table = jnp.where(same, table, -1)

        def onehot_step(step, carry):
            for s in range(4):
                i = step * 4 + s
                two = jnp.concatenate(
                    [
                        jnp.where(table == 2 * i, 1.0, 0.0),
                        jnp.where(table == 2 * i + 1, 1.0, 0.0),
                    ],
                    axis=0,
                ).astype(BF16)
                onehot[pl.ds(pl.multiple_of(i * 16, 16), 16), :] = two
            return carry

        lax.fori_loop(0, GROUPS * CG // 8, onehot_step, 0)
        loads[6].wait()

        def factor_step(chunk, carry):
            rows = pl.ds(pl.multiple_of(chunk * WIDE, WIDE), WIDE)
            raw = far_raw[pl.ds(chunk * CHUNK, CHUNK)].astype(F32)
            left_all[rows, :] = raw[:, 0].reshape(WIDE, PAD).astype(BF16)
            right_all[rows, :] = raw[:, 1].reshape(WIDE, PAD).astype(BF16)
            return carry

        lax.fori_loop(0, CHUNKS, factor_step, 0)

    def apply_operator(a, values):
        field = (field_first, field_second)[a]
        beside = (beside_first, beside_second)[a]
        for i in range(CG):
            packed = values[i].astype(BF16).astype(F32)
            low = values[i] - packed if a else jnp.zeros_like(packed)
            own_field[a, i] = jnp.concatenate([packed, low], axis=0)
            own_tiles[a, i] = fold(packed).astype(BF16)

        def send_field():
            for dz, to in zx_targets:
                if dz in NEAR_Z:
                    own, here = own_tiles.at[a], field.at[c * NZ + z, :, x]
                    send(own, here, send_sem.at[a, 0], agx_sem.at[a, z], to)
                else:
                    own, here = own_tiles.at[a, y], field.at[c * NZ + z, y, x]
                    send(own, here, send_sem.at[a, 2], agx_sem.at[a, z], to)
            for slot, target in ((0, above), (1, below)):
                to = beside.at[pl.ds(slot * CG, CG)]
                send(own_tiles.at[a], to, send_sem.at[a, 7], beside_sem.at[a], (target, y))
            field[c * NZ + z, :, x] = own_tiles[a]

        def far_out():
            own_rows = jnp.concatenate(
                [own_field[a, i, 0:RHS] for i in range(CG)], axis=0
            ).astype(BF16)

            def back_step(chunk, carry):
                rows = pl.ds(pl.multiple_of(chunk * WIDE, WIDE), WIDE)
                every = dot_nt(own_rows, left_all[rows, :])
                table = row_of[chunk]
                coef = jnp.zeros((RHS, WIDE), F32)
                for i in range(CG):
                    coef = coef + jnp.where(
                        table == i, every[i * RHS : (i + 1) * RHS], 0.0
                    )
                tall = jnp.concatenate([coef] * CHUNK, axis=0)
                tall = jnp.where(diagonal, tall, 0.0).astype(BF16)
                out = dot_nn(tall, right_all[rows, :])
                at = pl.ds(pl.multiple_of(chunk * CHUNK * RHS, CHUNK * RHS), CHUNK * RHS)
                far_back[a, at, :] = out.astype(BF16)
                return carry

            lax.fori_loop(0, CHUNKS, back_step, 0, unroll=True)

        def near_out():
            near_back[a] = jnp.zeros((3 * CG, RHS, PAD), F32)

            def near_back_step(step, carry):
                for s in range(UNROLL):
                    k = step * UNROLL + s
                    live = jnp.where(k < near_live, 1.0, 0.0)
                    out = dot_nn(own_field[a, pairs[0, k]].astype(BF16), near_blk[k])
                    out = out[:RHS] + out[RHS:]
                    column = pairs[1, k]
                    for j in range(3 * CG):
                        near_back[a, j] += out * jnp.where(column == j, live, 0.0)
                return carry

            lax.fori_loop(0, NEAR // UNROLL, near_back_step, 0)

        def spread_part(half, zz):
            block = half * NZ + zz
            rows = pl.ds(pl.multiple_of(block * PART * RHS, PART * RHS), PART * RHS)
            out = dot_nn(onehot[rows, :], far_back[a])
            return fold(out.reshape(PART, RHS, PAD))

        def theirs_step(j, carry):
            zz = far_to_near(j)
            spread[a, zz] = spread_part(1 - c, zz).astype(BF16)
            return carry

        def to_core_step(j, carry):
            zz = far_to_near(j)
            send(
                spread.at[a, zz], core_in.at[a, zz], send_sem.at[a, 1], rsc_sem.at[a, zz], core
            )
            return carry

        def ours_step(j, carry):
            zz = far_to_near(j)
            await_bytes(core_in.at[a, zz], rsc_sem.at[a, zz])
            total = spread_part(c, zz) + core_in[a, zz].astype(F32)
            x_out[a, zz] = total.reshape(NX, CG, 16, 128).astype(BF16)
            for o in x_others:
                send(
                    x_out.at[a, zz, o],
                    x_in.at[a, zz, x],
                    send_sem.at[a, 4],
                    rsx_sem.at[a, zz],
                    dev(xx=o),
                )
            return carry

        def along_y(d):
            zz = wrap(z + NZ - d, NZ)
            run = field.at[c * NZ + zz, y]
            await_bytes(run, agx_sem.at[a, zz])
            for target in y_targets:
                send(run, run, send_sem.at[a, 10], agy_sem.at[a, zz], target)

        def to_other_core(d):
            zz = wrap(z + NZ - d, NZ)
            slab = field.at[c * NZ + zz]
            if d in NEAR_Z:
                await_bytes(slab if d else field.at[0, pl.ds(0, NX - 1)], agx_sem.at[a, zz])
            else:
                await_bytes(field.at[0, pl.ds(0, NY - 1)], agy_sem.at[a, zz])
            send(slab, slab, send_sem.at[a, 3], agc_sem.at[a], core)

        if a == 0:
            prepare()
            far_out()
            lax.fori_loop(0, NZ, theirs_step, 0)
            pl.semaphore_wait(barrier, len(partners))
            send_field()
            lax.fori_loop(0, NZ, to_core_step, 0)
            lax.fori_loop(0, NZ, ours_step, 0)
        else:
            send_field()
            far_out()

            def both(j, carry):
                return to_core_step(j, theirs_step(j, carry))

            def all_three(j, carry):
                return ours_step(j, both(j + LAG, carry))

            lax.fori_loop(0, LAG, both, 0)
            lax.fori_loop(0, NZ - LAG, all_three, 0)
            lax.fori_loop(NZ - LAG, NZ, ours_step, 0)
        if a == 0:
            loads[7].wait()
            loads[8].wait()
        order = [0, 1, 7, 2, 6, 3, 5, 4]
        near_out()
        for first, slot, target in ((0, 1, below), (2 * CG, 0, above)):
            send(
                near_back.at[a, pl.ds(first, CG)],
                near_in.at[a, slot],
                send_sem.at[a, 8],
                near_sem.at[a],
                (target, y),
            )
        for d in (1, 7, 2, 6):
            along_y(d)
        await_bytes(beside, beside_sem.at[a])

        def near_step(step, sums):
            for s in range(UNROLL):
                k = step * UNROLL + s
                column = pairs[1, k]
                inside = lax.bitwise_and(column, CG - 1)
                own = jnp.logical_and(column >= CG, column < 2 * CG)
                tile = unfold(beside[jnp.where(column < CG, 0, CG) + inside].astype(F32))
                tile = jnp.concatenate([tile, jnp.zeros_like(tile)], axis=0)
                tile = jnp.where(own, own_field[a, inside], tile).astype(BF16)
                out = dot_nt(tile, near_blk[k])
                out = out[:RHS] + out[RHS:]
                row = pairs[0, k]
                live = jnp.where(k < near_live, 1.0, 0.0)
                sums = tuple(
                    sums[i] + out * jnp.where(row == i, live, 0.0) for i in range(CG)
                )
            return sums

        sums = tuple(near_back[a, CG + i] for i in range(CG))
        sums = lax.fori_loop(0, NEAR // UNROLL, near_step, sums)
        for d in (3, 5, 4):
            along_y(d)
        to_other_core(0)

        def x_sum_step(j):
            zz = far_to_near(j)
            await_bytes(x_in.at[a, zz, pl.ds(0, NX - 1)], rsx_sem.at[a, zz])
            x_in[a, zz, x] = x_out[a, zz, x]
            total = x_in[a, zz, 0].astype(F32)
            for o in range(1, NX):
                total = total + x_in[a, zz, o].astype(F32)
            z_out[a, zz] = total.astype(BF16)
            if j < NZ - 1:
                send(
                    z_out.at[a, zz], z_in.at[a, z], send_sem.at[a, 5], rsz_sem.at[a], dev(zz=zz)
                )

        for j in range(NZ):
            x_sum_step(j)
        for d in order[1:]:
            to_other_core(d)
        if a:
            share(0, [total_of([resid[i] * resid[i] for i in range(CG)])])

        await_bytes(field.at[pl.ds(0, NZ)], agc_sem.at[a])

        def forth_step(chunk, total):
            rows = pl.ds(pl.multiple_of(chunk * WIDE, WIDE), WIDE)
            tiles = [
                unfold(field[far_tile(chunk * CHUNK + s)].astype(F32))
                for s in range(CHUNK)
            ]
            tall = jnp.concatenate(tiles, axis=0).astype(BF16)
            every = jnp.where(diagonal, dot_nt(tall, right_all[rows, :]), 0.0)
            coef = jnp.sum(every.reshape(CHUNK, RHS, WIDE), axis=0)
            table = row_of[chunk]
            four = jnp.concatenate(
                [jnp.where(table == i, coef, 0.0) for i in range(CG)], axis=0
            )
            return total + dot_nn(four.astype(BF16), left_all[rows, :])

        far_rows = lax.fori_loop(
            0, CHUNKS, forth_step, jnp.zeros((CG * RHS, PAD), F32), unroll=True
        )
        self_out = dot_nt(own_field[a, y].astype(BF16), self_blk[0])
        self_out = self_out[:RHS] + self_out[RHS:]

        await_bytes(z_in.at[a, pl.ds(0, NZ - 1)], rsz_sem.at[a])
        z_in[a, z] = z_out[a, z]
        await_bytes(near_in.at[a], near_sem.at[a])
        for i in range(CG):
            total = near_in[a, 0, i] + near_in[a, 1, i]
            total = total + sums[i] + far_rows[i * RHS : (i + 1) * RHS]
            total = total + self_out * jnp.where(y == i, 1.0, 0.0)
            come = z_in[a, 0, i].astype(F32)
            for j in range(1, NZ):
                come = come + z_in[a, j, i].astype(F32)
            y_buf[a, y, i] = total + unfold(come)
        for target in y_targets:
            send(y_buf.at[a, y], y_buf.at[a, y], send_sem.at[a, 6], y_sem.at[a], target)
        if a:
            meanwhile()
        await_bytes(y_buf.at[a, pl.ds(0, NY - 1)], y_sem.at[a])
        return [
            valid[i] * (y_buf[a, 0, i] + y_buf[a, 1, i] + y_buf[a, 2, i] + y_buf[a, 3, i])
            for i in range(CG)
        ]

    sub = lax.broadcasted_iota(jnp.int32, (RHS, 128), 0)
    lane = lax.broadcasted_iota(jnp.int32, (RHS, 128), 1)

    def share(s, columns):
        spots = [
            jnp.where(lane == sub + p * RHS, column, 0.0) for p, column in enumerate(columns)
        ]
        row = functools.reduce(lambda p, q: p + q, spots)
        stats[s, pl.ds(me, 1)] = jnp.sum(row, axis=0, keepdims=True)
        part = stats.at[s, pl.ds(me, 1)]

        for target in everyone:
            send(part, part, send_sem.at[s, 9], stat_sem.at[s], target)

    def shared(s):
        await_bytes(stats.at[s, pl.ds(0, GROUPS - 1)], stat_sem.at[s])
        return stats[s]

    def column_of(row):
        tall = jnp.where(lane == sub, jnp.broadcast_to(row, (RHS, 128)), 0.0)
        return jnp.sum(tall, axis=1, keepdims=True)

    def total_of(tiles):
        return jnp.sum(
            functools.reduce(lambda p, q: p + q, tiles), axis=1, keepdims=True
        )

    def cut(ref, i):
        return ref[:, i * PAD : (i + 1) * PAD]

    initial = [cut(start_ref, i) * valid[i] for i in range(CG)]
    image = apply_operator(0, initial)
    loads[9].wait()
    for i in range(CG):
        resid[i] = cut(rhs_ref, i) * valid[i] - image[i]
    known = {}

    def meanwhile():
        square = jnp.sum(shared(0), axis=0, keepdims=True)
        known["norm"] = jnp.sqrt(square / PANELS + EPSILON)
        column = column_of(known["norm"])
        known["column"] = column
        known["basis"] = [resid[i] / column for i in range(CG)]
        known["size"] = total_of([v * v for v in known["basis"]])

    image = apply_operator(1, [resid[i] for i in range(CG)])
    start_norm, basis, size = known["norm"], known["basis"], known["size"]
    image = [image[i] / known["column"] for i in range(CG)]
    inner = total_of([basis[i] * image[i] for i in range(CG)])
    centre = ratio(inner, size)
    rest = [image[i] - centre * basis[i] for i in range(CG)]
    share(1, [inner, size, total_of([rest[i] * rest[i] for i in range(CG)])])

    inner = shared(1)
    size = pltpu.roll(inner, 128 - RHS, 1)
    rest = pltpu.roll(inner, 128 - 2 * RHS, 1)
    inner_all = jnp.sum(inner, axis=0, keepdims=True)
    h_diag = inner_all / PANELS
    below_square = jnp.sum(about(inner, size, rest, h_diag), axis=0, keepdims=True)
    h_below = jnp.sqrt(jnp.maximum(below_square, 0.0) / PANELS + EPSILON)
    denominator = h_diag * h_diag + h_below * h_below
    step_size = column_of(start_norm * h_diag / denominator)
    norm_ref[...] = start_norm * h_below / jnp.sqrt(denominator)
    diag_column = column_of(h_diag)
    below_column = column_of(h_below)
    for i in range(CG):
        pair_ref[0, :, i * PAD : (i + 1) * PAD] = (
            cut(start_ref, i) * valid[i] + step_size * basis[i]
        )
        pair_ref[1, :, i * PAD : (i + 1) * PAD] = (
            image[i] - diag_column * basis[i]
        ) / below_column

    for a in range(2):
        field = (field_first, field_second)[a]
        await_bytes(spread.at[a], send_sem.at[a, 1])
        await_bytes(field.at[0, pl.ds(0, NX - 1)], send_sem.at[a, 0])
        await_bytes(field.at[pl.ds(0, 1), pl.ds(0, CG)], send_sem.at[a, 2])
        await_bytes(field.at[0, pl.ds(0, 3)], send_sem.at[a, 2])
        await_bytes(field.at[pl.ds(0, NZ - 1), pl.ds(0, NY - 1)], send_sem.at[a, 10])
        await_bytes(field.at[pl.ds(0, NZ)], send_sem.at[a, 3])
        await_bytes(x_in.at[a, pl.ds(0, NZ), pl.ds(0, NX - 1)], send_sem.at[a, 4])
        await_bytes(z_in.at[a, pl.ds(0, NZ - 1)], send_sem.at[a, 5])
        await_bytes(y_buf.at[a, pl.ds(0, NY - 1)], send_sem.at[a, 6])
        await_bytes(field.at[0, pl.ds(0, 2)], send_sem.at[a, 7])
        await_bytes(near_in.at[a], send_sem.at[a, 8])
        await_bytes(stats.at[a, pl.ds(0, GROUPS - 1)], send_sem.at[a, 9])


def local(
    right_side,
    start,
    cluster_sizes,
    self_blocks,
    near_blocks,
    near_pairs,
    far_factors,
    far_group,
    far_local,
    block_counts,
):
    vmem = pl.BlockSpec(memory_space=pltpu.VMEM)
    hbm = pl.BlockSpec(memory_space=pl.ANY)
    dma = pltpu.SemaphoreType.DMA
    wide = (RHS, CG * PAD)
    both, norm = pl.pallas_call(
        kernel,
        out_shape=(
            jax.ShapeDtypeStruct((2,) + wide, F32),
            jax.ShapeDtypeStruct((1, 128), F32),
        ),
        in_specs=[hbm] * 10,
        out_specs=(vmem, vmem),
        scratch_shapes=[
            pltpu.SMEM((1, 2), jnp.int32),
            pltpu.SMEM((2, NEAR), jnp.int32),
            pltpu.SMEM((1, FAR), jnp.int32),
            pltpu.SMEM((2, FAR), jnp.int32),
            pltpu.SMEM((CG,), jnp.int32),
            pltpu.VMEM(wide, F32),
            pltpu.VMEM(wide, F32),
            pltpu.VMEM((1, PAD, PAD), BF16),
            pltpu.VMEM((NEAR, PAD, PAD), BF16),
            pltpu.VMEM((FAR, 2, RANK, PAD), BF16),
            pltpu.VMEM((FAR * RANK, PAD), BF16),
            pltpu.VMEM((FAR * RANK, PAD), BF16),
            pltpu.VMEM((GROUPS * CG * RHS, FAR * RHS), BF16),
            pltpu.VMEM((CHUNKS, RHS, WIDE), jnp.int32),
            pltpu.VMEM((NC * NZ, CG, NX, 16, 128), BF16),
            pltpu.VMEM((NC * NZ, CG, NX, 16, 128), BF16),
            pltpu.VMEM((2 * CG, 16, 128), BF16),
            pltpu.VMEM((2 * CG, 16, 128), BF16),
            pltpu.VMEM((2, CG, 2 * RHS, PAD), F32),
            pltpu.VMEM((2, CG, 16, 128), BF16),
            pltpu.VMEM((2, FAR * RHS, PAD), BF16),
            pltpu.VMEM((2, 3 * CG, RHS, PAD), F32),
            pltpu.VMEM((2, 2, CG, RHS, PAD), F32),
            pltpu.VMEM((2, NZ, PART, 16, 128), BF16),
            pltpu.VMEM((2, NZ, PART, 16, 128), BF16),
            pltpu.VMEM((2, NZ, NX, CG, 16, 128), BF16),
            pltpu.VMEM((2, NZ, NX, CG, 16, 128), BF16),
            pltpu.VMEM((2, NZ, CG, 16, 128), BF16),
            pltpu.VMEM((2, NZ, CG, 16, 128), BF16),
            pltpu.VMEM((2, NY, CG, RHS, PAD), F32),
            pltpu.VMEM((CG, RHS, PAD), F32),
            pltpu.VMEM((2, GROUPS, 128), F32),
            dma((10,)),
            dma((2, 11)),
            dma((2, NZ - 1)),
            dma((2, NZ)),
            dma((2, NZ)),
            dma((2,)),
            dma((2, NZ)),
            dma((2, NZ)),
            dma((2,)),
            dma((2,)),
            dma((2,)),
            dma((2,)),
            dma((2,)),
        ],
        compiler_params=pltpu.CompilerParams(
            collective_id=0, has_side_effects=True, vmem_limit_bytes=60 * 1024 * 1024
        ),
    )(
        block_counts,
        near_pairs.T,
        far_group.T,
        far_local.T,
        cluster_sizes,
        right_side,
        start,
        self_blocks,
        near_blocks,
        far_factors,
    )
    return both[0], both[1], norm[0, :RHS]


def solution(mesh):
    in_specs = (
        P(None, "clus"),
        P(None, "clus"),
        P("clus"),
        P(("clus", "pair"), None, None),
        P(("clus", "pair"), None, None),
        P(("clus", "pair"), None),
        P(("clus", "pair"), None, None, None),
        P(("clus", "pair"), None),
        P(("clus", "pair"), None),
        P(("clus", "pair"), None),
    )
    out_specs = (P(None, "clus"), P(None, "clus"), P())
    return jax.shard_map(local, mesh=mesh, in_specs=in_specs, out_specs=out_specs, check_vma=False)
```

```python
import functools

import jax
import jax.numpy as jnp
from jax import lax
from jax.experimental import pallas as pl
from jax.experimental.pallas import tpu as pltpu
from jax.sharding import PartitionSpec as P

PAD = 256
RHS = 8
CG = 4
RANK = 24
NZ, NX, NC, NY = 8, 4, 2, 4
GROUPS = NZ * NX * NC
PANELS = GROUPS * CG * PAD
NEAR = 16
FAR = 64
CHUNK = 16
CHUNKS = FAR // CHUNK
WIDE = CHUNK * RANK
HALF = NZ * NX * CG
PART = NX * CG
NEAR_Z = (0,)
LAG = 3
UNROLL = 16

EPSILON = 1e-06
F32 = jnp.float32
BF16 = jnp.bfloat16

def fold(tile):
    return jnp.concatenate([tile[..., :128], tile[..., 128:]], axis=-2)


def unfold(tile):
    return jnp.concatenate([tile[..., :RHS, :], tile[..., RHS:, :]], axis=-1)


def dot_nt(a, b):
    return lax.dot_general(a, b, (((1,), (1,)), ((), ())), preferred_element_type=F32)


def dot_nn(a, b):
    return lax.dot_general(a, b, (((1,), (0,)), ((), ())), preferred_element_type=F32)


def ratio(a, n):
    ok = n > 1e-30
    return jnp.where(ok, a / jnp.where(ok, n, 1.0), 0.0)


def about(a, n, s, centre):
    own = ratio(a, n)
    off = own - centre
    return s + 2.0 * off * (a - own * n) + off * off * n


def kernel(
    counts_hbm,
    pairs_hbm,
    group_hbm,
    local_hbm,
    sizes_hbm,
    rhs_hbm,
    start_hbm,
    self_hbm,
    near_hbm,
    far_hbm,
    pair_ref,
    norm_ref,
    counts,
    pairs,
    groups,
    locals_,
    sizes,
    rhs_ref,
    start_ref,
    self_blk,
    near_blk,
    far_raw,
    left_all,
    right_all,
    onehot,
    row_of,
    field_first,
    field_second,
    beside_first,
    beside_second,
    own_field,
    own_tiles,
    far_back,
    near_back,
    near_in,
    spread,
    core_in,
    x_out,
    x_in,
    z_out,
    z_in,
    y_buf,
    resid,
    stats,
    load_sem,
    send_sem,
    agz_sem,
    agx_sem,
    agy_sem,
    agc_sem,
    rsc_sem,
    rsx_sem,
    rsz_sem,
    y_sem,
    beside_sem,
    near_sem,
    stat_sem,
):
    me = lax.axis_index("clus")
    y = lax.axis_index("pair")
    z = lax.shift_right_logical(me, 3)
    x = lax.bitwise_and(lax.shift_right_logical(me, 1), NX - 1)
    c = lax.bitwise_and(me, NC - 1)

    loads = [
        pltpu.make_async_copy(src, dst, load_sem.at[i])
        for i, (src, dst) in enumerate(
            [
                (counts_hbm, counts),
                (pairs_hbm, pairs),
                (group_hbm, groups),
                (local_hbm, locals_),
                (sizes_hbm, sizes),
                (start_hbm, start_ref),
                (far_hbm, far_raw),
                (near_hbm, near_blk),
                (self_hbm, self_blk),
                (rhs_hbm, rhs_ref),
            ]
        )
    ]
    for load in loads:
        load.start()

    def wrap(value, size):
        return lax.bitwise_and(value, size - 1)

    def dev(zz=None, xx=None, cc=None, yy=None):
        zz = z if zz is None else zz
        xx = x if xx is None else xx
        cc = c if cc is None else cc
        yy = y if yy is None else yy
        return ((zz * NX + xx) * NC + cc, yy)

    def send(src, dst, ssem, rsem, target):
        pltpu.make_async_remote_copy(
            src_ref=src,
            dst_ref=dst,
            send_sem=ssem,
            recv_sem=rsem,
            device_id=target,
            device_id_type=pl.DeviceIdType.MESH,
        ).start()

    def await_bytes(ref, sem):
        pltpu.make_async_copy(ref, ref, sem).wait()

    x_others = [wrap(x + d, NX) for d in (2, 1, 3)]
    x_targets = [dev(xx=o) for o in x_others]
    y_targets = [dev(yy=wrap(y + d, NY)) for d in (2, 1, 3)]
    core = dev(cc=1 - c)
    below = wrap(me + GROUPS - 1, GROUPS)
    above = wrap(me + 1, GROUPS)
    def hops(place):
        dz, dx, dc = place
        return min(dz, NZ - dz) + min(dx, NX - dx) + 0.5 * dc

    places = [(i, j, k) for i in range(NZ) for j in range(NX) for k in range(NC)]
    everyone = [
        dev(zz=wrap(z + i, NZ), xx=wrap(x + j, NX), cc=wrap(c + k, NC))
        for i, j, k in sorted(places, key=hops, reverse=True)
        if i or j or k
    ]
    zx_targets = [
        (dz, dev(zz=wrap(z + dz, NZ), xx=wrap(x + dx, NX)))
        for dz in (4, 3, 5, 2, 6, 1, 7, 0)
        for dx in (2, 1, 3, 0)
        if dz or dx
    ]
    partners = [target for _, target in zx_targets] + y_targets + [core, (below, y), (above, y)]

    barrier = pltpu.get_barrier_semaphore()
    for target in partners:
        pl.semaphore_signal(
            barrier, inc=1, device_id=target, device_id_type=pl.DeviceIdType.MESH
        )

    for load in loads[:6]:
        load.wait()
    lane = lax.broadcasted_iota(jnp.int32, (RHS, PAD), 1)
    valid = [(lane < sizes[i]).astype(F32) for i in range(CG)]
    near_live = counts[0, 0]
    far_live = counts[0, 1]


    def far_place(k):
        group = groups[0, k]
        return (
            lax.bitwise_and(group, 1) * HALF
            + lax.shift_right_logical(group, 1) * CG
            + locals_[1, k]
        )

    def far_tile(k):
        group = groups[0, k]
        return (
            lax.bitwise_and(group, 1) * NZ + lax.shift_right_logical(group, 3),
            locals_[1, k],
            lax.bitwise_and(lax.shift_right_logical(group, 1), NX - 1),
        )

    diagonal = (
        lax.broadcasted_iota(jnp.int32, (CHUNK * RHS, WIDE), 0) // RHS
        == lax.broadcasted_iota(jnp.int32, (CHUNK * RHS, WIDE), 1) // RANK
    )

    def far_to_near(j):
        odd = j % 2
        return wrap(z + NZ // 2 + (1 - 2 * odd) * ((j + 1) // 2), NZ)

    def prepare():
        slot = lax.broadcasted_iota(jnp.int32, (RHS, WIDE), 1) // RANK

        def rows_step(chunk, carry):
            table = jnp.full((RHS, WIDE), -1, jnp.int32)
            for s in range(CHUNK):
                k = chunk * CHUNK + s
                row = jnp.where(k < far_live, locals_[0, k], -1)
                table = jnp.where(slot == s, row, table)
            row_of[chunk] = table
            return carry

        lax.fori_loop(0, CHUNKS, rows_step, 0)

        wide = lax.broadcasted_iota(jnp.int32, (RHS, FAR * RHS), 1)
        slot_of = wide // RHS

        def place_step(step, table):
            for s in range(8):
                k = step * 8 + s
                table = jnp.where(slot_of == k, far_place(k), table)
            return table

        table = lax.fori_loop(
            0, FAR // 8, place_step, jnp.full((RHS, FAR * RHS), -1, jnp.int32)
        )
        same = lax.broadcasted_iota(jnp.int32, (RHS, FAR * RHS), 0) == wide % RHS
        table = jnp.where(same, table, -1)

        def onehot_step(step, carry):
            for s in range(4):
                i = step * 4 + s
                two = jnp.concatenate(
                    [
                        jnp.where(table == 2 * i, 1.0, 0.0),
                        jnp.where(table == 2 * i + 1, 1.0, 0.0),
                    ],
                    axis=0,
                ).astype(BF16)
                onehot[pl.ds(pl.multiple_of(i * 16, 16), 16), :] = two
            return carry

        lax.fori_loop(0, GROUPS * CG // 8, onehot_step, 0)
        loads[6].wait()

        def factor_step(chunk, carry):
            rows = pl.ds(pl.multiple_of(chunk * WIDE, WIDE), WIDE)
            raw = far_raw[pl.ds(chunk * CHUNK, CHUNK)].astype(F32)
            left_all[rows, :] = raw[:, 0].reshape(WIDE, PAD).astype(BF16)
            right_all[rows, :] = raw[:, 1].reshape(WIDE, PAD).astype(BF16)
            return carry

        lax.fori_loop(0, CHUNKS, factor_step, 0)

    def apply_operator(a, values):
        field = (field_first, field_second)[a]
        beside = (beside_first, beside_second)[a]
        for i in range(CG):
            packed = values[i].astype(BF16).astype(F32)
            low = values[i] - packed if a else jnp.zeros_like(packed)
            own_field[a, i] = jnp.concatenate([packed, low], axis=0)
            own_tiles[a, i] = fold(packed).astype(BF16)

        def send_field():
            for dz, to in zx_targets:
                if dz in NEAR_Z:
                    own, here = own_tiles.at[a], field.at[c * NZ + z, :, x]
                    send(own, here, send_sem.at[a, 0], agx_sem.at[a, z], to)
                else:
                    own, here = own_tiles.at[a, y], field.at[c * NZ + z, y, x]
                    send(own, here, send_sem.at[a, 2], agx_sem.at[a, z], to)
            for slot, target in ((0, above), (1, below)):
                to = beside.at[pl.ds(slot * CG, CG)]
                send(own_tiles.at[a], to, send_sem.at[a, 7], beside_sem.at[a], (target, y))
            field[c * NZ + z, :, x] = own_tiles[a]

        def far_out():
            own_rows = jnp.concatenate(
                [own_field[a, i, 0:RHS] for i in range(CG)], axis=0
            ).astype(BF16)

            def back_step(chunk, carry):
                rows = pl.ds(pl.multiple_of(chunk * WIDE, WIDE), WIDE)
                every = dot_nt(own_rows, left_all[rows, :])
                table = row_of[chunk]
                coef = jnp.zeros((RHS, WIDE), F32)
                for i in range(CG):
                    coef = coef + jnp.where(
                        table == i, every[i * RHS : (i + 1) * RHS], 0.0
                    )
                tall = jnp.concatenate([coef] * CHUNK, axis=0)
                tall = jnp.where(diagonal, tall, 0.0).astype(BF16)
                out = dot_nn(tall, right_all[rows, :])
                at = pl.ds(pl.multiple_of(chunk * CHUNK * RHS, CHUNK * RHS), CHUNK * RHS)
                far_back[a, at, :] = out.astype(BF16)
                return carry

            lax.fori_loop(0, CHUNKS, back_step, 0, unroll=True)

        def near_out():
            near_back[a] = jnp.zeros((3 * CG, RHS, PAD), F32)

            def near_back_step(step, carry):
                for s in range(UNROLL):
                    k = step * UNROLL + s
                    live = jnp.where(k < near_live, 1.0, 0.0)
                    out = dot_nn(own_field[a, pairs[0, k]].astype(BF16), near_blk[k])
                    out = out[:RHS] + out[RHS:]
                    column = pairs[1, k]
                    for j in range(3 * CG):
                        near_back[a, j] += out * jnp.where(column == j, live, 0.0)
                return carry

            lax.fori_loop(0, NEAR // UNROLL, near_back_step, 0)

        def spread_part(half, zz):
            block = half * NZ + zz
            rows = pl.ds(pl.multiple_of(block * PART * RHS, PART * RHS), PART * RHS)
            out = dot_nn(onehot[rows, :], far_back[a])
            return fold(out.reshape(PART, RHS, PAD))

        def theirs_step(j, carry):
            zz = far_to_near(j)
            spread[a, zz] = spread_part(1 - c, zz).astype(BF16)
            return carry

        def to_core_step(j, carry):
            zz = far_to_near(j)
            send(
                spread.at[a, zz], core_in.at[a, zz], send_sem.at[a, 1], rsc_sem.at[a, zz], core
            )
            return carry

        def ours_step(j, carry):
            zz = far_to_near(j)
            await_bytes(core_in.at[a, zz], rsc_sem.at[a, zz])
            total = spread_part(c, zz) + core_in[a, zz].astype(F32)
            x_out[a, zz] = total.reshape(NX, CG, 16, 128).astype(BF16)
            for o in x_others:
                send(
                    x_out.at[a, zz, o],
                    x_in.at[a, zz, x],
                    send_sem.at[a, 4],
                    rsx_sem.at[a, zz],
                    dev(xx=o),
                )
            return carry

        def along_y(d):
            zz = wrap(z + NZ - d, NZ)
            run = field.at[c * NZ + zz, y]
            await_bytes(run, agx_sem.at[a, zz])
            for target in y_targets:
                send(run, run, send_sem.at[a, 10], agy_sem.at[a, zz], target)

        def to_other_core(d):
            zz = wrap(z + NZ - d, NZ)
            slab = field.at[c * NZ + zz]
            if d in NEAR_Z:
                await_bytes(slab if d else field.at[0, pl.ds(0, NX - 1)], agx_sem.at[a, zz])
            else:
                await_bytes(field.at[0, pl.ds(0, NY - 1)], agy_sem.at[a, zz])
            send(slab, slab, send_sem.at[a, 3], agc_sem.at[a], core)

        if a == 0:
            prepare()
            far_out()
            lax.fori_loop(0, NZ, theirs_step, 0, unroll=True)
            pl.semaphore_wait(barrier, len(partners))
            send_field()
            lax.fori_loop(0, NZ, to_core_step, 0, unroll=True)
            lax.fori_loop(0, NZ, ours_step, 0, unroll=True)
        else:
            send_field()
            far_out()

            def both(j, carry):
                return to_core_step(j, theirs_step(j, carry))

            def all_three(j, carry):
                return ours_step(j, both(j + LAG, carry))

            lax.fori_loop(0, LAG, both, 0, unroll=True)
            lax.fori_loop(0, NZ - LAG, all_three, 0, unroll=True)
            lax.fori_loop(NZ - LAG, NZ, ours_step, 0, unroll=True)
        if a == 0:
            loads[7].wait()
            loads[8].wait()
        order = [0, 1, 7, 2, 6, 3, 5, 4]
        near_out()
        for first, slot, target in ((0, 1, below), (2 * CG, 0, above)):
            send(
                near_back.at[a, pl.ds(first, CG)],
                near_in.at[a, slot],
                send_sem.at[a, 8],
                near_sem.at[a],
                (target, y),
            )
        for d in (1, 7, 2, 6):
            along_y(d)
        await_bytes(beside, beside_sem.at[a])

        def near_step(step, sums):
            for s in range(UNROLL):
                k = step * UNROLL + s
                column = pairs[1, k]
                inside = lax.bitwise_and(column, CG - 1)
                own = jnp.logical_and(column >= CG, column < 2 * CG)
                tile = unfold(beside[jnp.where(column < CG, 0, CG) + inside].astype(F32))
                tile = jnp.concatenate([tile, jnp.zeros_like(tile)], axis=0)
                tile = jnp.where(own, own_field[a, inside], tile).astype(BF16)
                out = dot_nt(tile, near_blk[k])
                out = out[:RHS] + out[RHS:]
                row = pairs[0, k]
                live = jnp.where(k < near_live, 1.0, 0.0)
                sums = tuple(
                    sums[i] + out * jnp.where(row == i, live, 0.0) for i in range(CG)
                )
            return sums

        sums = tuple(near_back[a, CG + i] for i in range(CG))
        sums = lax.fori_loop(0, NEAR // UNROLL, near_step, sums)
        for d in (3, 5, 4):
            along_y(d)
        to_other_core(0)

        def x_sum_step(j):
            zz = far_to_near(j)
            await_bytes(x_in.at[a, zz, pl.ds(0, NX - 1)], rsx_sem.at[a, zz])
            x_in[a, zz, x] = x_out[a, zz, x]
            total = x_in[a, zz, 0].astype(F32)
            for o in range(1, NX):
                total = total + x_in[a, zz, o].astype(F32)
            z_out[a, zz] = total.astype(BF16)
            if j < NZ - 1:
                send(
                    z_out.at[a, zz], z_in.at[a, z], send_sem.at[a, 5], rsz_sem.at[a], dev(zz=zz)
                )

        for j in range(NZ):
            x_sum_step(j)
        for d in order[1:]:
            to_other_core(d)
        if a:
            share(0, [total_of([resid[i] * resid[i] for i in range(CG)])])

        await_bytes(field.at[pl.ds(0, NZ)], agc_sem.at[a])

        def forth_step(chunk, total):
            rows = pl.ds(pl.multiple_of(chunk * WIDE, WIDE), WIDE)
            tiles = [
                unfold(field[far_tile(chunk * CHUNK + s)].astype(F32))
                for s in range(CHUNK)
            ]
            tall = jnp.concatenate(tiles, axis=0).astype(BF16)
            every = jnp.where(diagonal, dot_nt(tall, right_all[rows, :]), 0.0)
            coef = jnp.sum(every.reshape(CHUNK, RHS, WIDE), axis=0)
            table = row_of[chunk]
            four = jnp.concatenate(
                [jnp.where(table == i, coef, 0.0) for i in range(CG)], axis=0
            )
            return total + dot_nn(four.astype(BF16), left_all[rows, :])

        far_rows = lax.fori_loop(
            0, CHUNKS, forth_step, jnp.zeros((CG * RHS, PAD), F32), unroll=True
        )
        self_out = dot_nt(own_field[a, y].astype(BF16), self_blk[0])
        self_out = self_out[:RHS] + self_out[RHS:]

        await_bytes(z_in.at[a, pl.ds(0, NZ - 1)], rsz_sem.at[a])
        z_in[a, z] = z_out[a, z]
        await_bytes(near_in.at[a], near_sem.at[a])
        for i in range(CG):
            total = near_in[a, 0, i] + near_in[a, 1, i]
            total = total + sums[i] + far_rows[i * RHS : (i + 1) * RHS]
            total = total + self_out * jnp.where(y == i, 1.0, 0.0)
            come = z_in[a, 0, i].astype(F32)
            for j in range(1, NZ):
                come = come + z_in[a, j, i].astype(F32)
            y_buf[a, y, i] = total + unfold(come)
        for target in y_targets:
            send(y_buf.at[a, y], y_buf.at[a, y], send_sem.at[a, 6], y_sem.at[a], target)
        if a:
            meanwhile()
        await_bytes(y_buf.at[a, pl.ds(0, NY - 1)], y_sem.at[a])
        return [
            valid[i] * (y_buf[a, 0, i] + y_buf[a, 1, i] + y_buf[a, 2, i] + y_buf[a, 3, i])
            for i in range(CG)
        ]

    sub = lax.broadcasted_iota(jnp.int32, (RHS, 128), 0)
    lane = lax.broadcasted_iota(jnp.int32, (RHS, 128), 1)

    def share(s, columns):
        spots = [
            jnp.where(lane == sub + p * RHS, column, 0.0) for p, column in enumerate(columns)
        ]
        row = functools.reduce(lambda p, q: p + q, spots)
        stats[s, pl.ds(me, 1)] = jnp.sum(row, axis=0, keepdims=True)
        part = stats.at[s, pl.ds(me, 1)]

        for target in everyone:
            send(part, part, send_sem.at[s, 9], stat_sem.at[s], target)

    def shared(s):
        await_bytes(stats.at[s, pl.ds(0, GROUPS - 1)], stat_sem.at[s])
        return stats[s]

    def column_of(row):
        tall = jnp.where(lane == sub, jnp.broadcast_to(row, (RHS, 128)), 0.0)
        return jnp.sum(tall, axis=1, keepdims=True)

    def total_of(tiles):
        return jnp.sum(
            functools.reduce(lambda p, q: p + q, tiles), axis=1, keepdims=True
        )

    def cut(ref, i):
        return ref[:, i * PAD : (i + 1) * PAD]

    initial = [cut(start_ref, i) * valid[i] for i in range(CG)]
    image = apply_operator(0, initial)
    loads[9].wait()
    for i in range(CG):
        resid[i] = cut(rhs_ref, i) * valid[i] - image[i]
    known = {}

    def meanwhile():
        square = jnp.sum(shared(0), axis=0, keepdims=True)
        known["norm"] = jnp.sqrt(square / PANELS + EPSILON)
        column = column_of(known["norm"])
        known["column"] = column
        known["basis"] = [resid[i] / column for i in range(CG)]
        known["size"] = total_of([v * v for v in known["basis"]])

    image = apply_operator(1, [resid[i] for i in range(CG)])
    start_norm, basis, size = known["norm"], known["basis"], known["size"]
    image = [image[i] / known["column"] for i in range(CG)]
    inner = total_of([basis[i] * image[i] for i in range(CG)])
    centre = ratio(inner, size)
    rest = [image[i] - centre * basis[i] for i in range(CG)]
    share(1, [inner, size, total_of([rest[i] * rest[i] for i in range(CG)])])

    inner = shared(1)
    size = pltpu.roll(inner, 128 - RHS, 1)
    rest = pltpu.roll(inner, 128 - 2 * RHS, 1)
    inner_all = jnp.sum(inner, axis=0, keepdims=True)
    h_diag = inner_all / PANELS
    below_square = jnp.sum(about(inner, size, rest, h_diag), axis=0, keepdims=True)
    h_below = jnp.sqrt(jnp.maximum(below_square, 0.0) / PANELS + EPSILON)
    denominator = h_diag * h_diag + h_below * h_below
    step_size = column_of(start_norm * h_diag / denominator)
    norm_ref[...] = start_norm * h_below / jnp.sqrt(denominator)
    diag_column = column_of(h_diag)
    below_column = column_of(h_below)
    for i in range(CG):
        pair_ref[0, :, i * PAD : (i + 1) * PAD] = (
            cut(start_ref, i) * valid[i] + step_size * basis[i]
        )
        pair_ref[1, :, i * PAD : (i + 1) * PAD] = (
            image[i] - diag_column * basis[i]
        ) / below_column

    for a in range(2):
        field = (field_first, field_second)[a]
        await_bytes(spread.at[a], send_sem.at[a, 1])
        await_bytes(field.at[0, pl.ds(0, NX - 1)], send_sem.at[a, 0])
        await_bytes(field.at[pl.ds(0, 1), pl.ds(0, CG)], send_sem.at[a, 2])
        await_bytes(field.at[0, pl.ds(0, 3)], send_sem.at[a, 2])
        await_bytes(field.at[pl.ds(0, NZ - 1), pl.ds(0, NY - 1)], send_sem.at[a, 10])
        await_bytes(field.at[pl.ds(0, NZ)], send_sem.at[a, 3])
        await_bytes(x_in.at[a, pl.ds(0, NZ), pl.ds(0, NX - 1)], send_sem.at[a, 4])
        await_bytes(z_in.at[a, pl.ds(0, NZ - 1)], send_sem.at[a, 5])
        await_bytes(y_buf.at[a, pl.ds(0, NY - 1)], send_sem.at[a, 6])
        await_bytes(field.at[0, pl.ds(0, 2)], send_sem.at[a, 7])
        await_bytes(near_in.at[a], send_sem.at[a, 8])
        await_bytes(stats.at[a, pl.ds(0, GROUPS - 1)], send_sem.at[a, 9])


def local(
    right_side,
    start,
    cluster_sizes,
    self_blocks,
    near_blocks,
    near_pairs,
    far_factors,
    far_group,
    far_local,
    block_counts,
):
    vmem = pl.BlockSpec(memory_space=pltpu.VMEM)
    hbm = pl.BlockSpec(memory_space=pl.ANY)
    dma = pltpu.SemaphoreType.DMA
    wide = (RHS, CG * PAD)
    both, norm = pl.pallas_call(
        kernel,
        out_shape=(
            jax.ShapeDtypeStruct((2,) + wide, F32),
            jax.ShapeDtypeStruct((1, 128), F32),
        ),
        in_specs=[hbm] * 10,
        out_specs=(vmem, vmem),
        scratch_shapes=[
            pltpu.SMEM((1, 2), jnp.int32),
            pltpu.SMEM((2, NEAR), jnp.int32),
            pltpu.SMEM((1, FAR), jnp.int32),
            pltpu.SMEM((2, FAR), jnp.int32),
            pltpu.SMEM((CG,), jnp.int32),
            pltpu.VMEM(wide, F32),
            pltpu.VMEM(wide, F32),
            pltpu.VMEM((1, PAD, PAD), BF16),
            pltpu.VMEM((NEAR, PAD, PAD), BF16),
            pltpu.VMEM((FAR, 2, RANK, PAD), BF16),
            pltpu.VMEM((FAR * RANK, PAD), BF16),
            pltpu.VMEM((FAR * RANK, PAD), BF16),
            pltpu.VMEM((GROUPS * CG * RHS, FAR * RHS), BF16),
            pltpu.VMEM((CHUNKS, RHS, WIDE), jnp.int32),
            pltpu.VMEM((NC * NZ, CG, NX, 16, 128), BF16),
            pltpu.VMEM((NC * NZ, CG, NX, 16, 128), BF16),
            pltpu.VMEM((2 * CG, 16, 128), BF16),
            pltpu.VMEM((2 * CG, 16, 128), BF16),
            pltpu.VMEM((2, CG, 2 * RHS, PAD), F32),
            pltpu.VMEM((2, CG, 16, 128), BF16),
            pltpu.VMEM((2, FAR * RHS, PAD), BF16),
            pltpu.VMEM((2, 3 * CG, RHS, PAD), F32),
            pltpu.VMEM((2, 2, CG, RHS, PAD), F32),
            pltpu.VMEM((2, NZ, PART, 16, 128), BF16),
            pltpu.VMEM((2, NZ, PART, 16, 128), BF16),
            pltpu.VMEM((2, NZ, NX, CG, 16, 128), BF16),
            pltpu.VMEM((2, NZ, NX, CG, 16, 128), BF16),
            pltpu.VMEM((2, NZ, CG, 16, 128), BF16),
            pltpu.VMEM((2, NZ, CG, 16, 128), BF16),
            pltpu.VMEM((2, NY, CG, RHS, PAD), F32),
            pltpu.VMEM((CG, RHS, PAD), F32),
            pltpu.VMEM((2, GROUPS, 128), F32),
            dma((10,)),
            dma((2, 11)),
            dma((2, NZ - 1)),
            dma((2, NZ)),
            dma((2, NZ)),
            dma((2,)),
            dma((2, NZ)),
            dma((2, NZ)),
            dma((2,)),
            dma((2,)),
            dma((2,)),
            dma((2,)),
            dma((2,)),
        ],
        compiler_params=pltpu.CompilerParams(
            collective_id=0, has_side_effects=True, vmem_limit_bytes=60 * 1024 * 1024
        ),
    )(
        block_counts,
        near_pairs.T,
        far_group.T,
        far_local.T,
        cluster_sizes,
        right_side,
        start,
        self_blocks,
        near_blocks,
        far_factors,
    )
    return both[0], both[1], norm[0, :RHS]


def solution(mesh):
    in_specs = (
        P(None, "clus"),
        P(None, "clus"),
        P("clus"),
        P(("clus", "pair"), None, None),
        P(("clus", "pair"), None, None),
        P(("clus", "pair"), None),
        P(("clus", "pair"), None, None, None),
        P(("clus", "pair"), None),
        P(("clus", "pair"), None),
        P(("clus", "pair"), None),
    )
    out_specs = (P(None, "clus"), P(None, "clus"), P())
    return jax.shard_map(local, mesh=mesh, in_specs=in_specs, out_specs=out_specs, check_vma=False)
```

```python
import functools

import jax
import jax.numpy as jnp
from jax import lax
from jax.experimental import pallas as pl
from jax.experimental.pallas import tpu as pltpu
from jax.sharding import PartitionSpec as P

PAD = 256
RHS = 8
CG = 4
RANK = 24
NZ, NX, NC, NY = 8, 4, 2, 4
GROUPS = NZ * NX * NC
PANELS = GROUPS * CG * PAD
NEAR = 16
FAR = 64
CHUNK = 16
CHUNKS = FAR // CHUNK
WIDE = CHUNK * RANK
HALF = NZ * NX * CG
PART = NX * CG
NEAR_Z = (0,)
LAG = 3
UNROLL = 16

EPSILON = 1e-06
F32 = jnp.float32
BF16 = jnp.bfloat16

def fold(tile):
    return jnp.concatenate([tile[..., :128], tile[..., 128:]], axis=-2)


def unfold(tile):
    return jnp.concatenate([tile[..., :RHS, :], tile[..., RHS:, :]], axis=-1)


def dot_nt(a, b):
    return lax.dot_general(a, b, (((1,), (1,)), ((), ())), preferred_element_type=F32)


def dot_nn(a, b):
    return lax.dot_general(a, b, (((1,), (0,)), ((), ())), preferred_element_type=F32)


def ratio(a, n):
    ok = n > 1e-30
    return jnp.where(ok, a / jnp.where(ok, n, 1.0), 0.0)


def about(a, n, s, centre):
    own = ratio(a, n)
    off = own - centre
    return s + 2.0 * off * (a - own * n) + off * off * n


def kernel(
    counts_hbm,
    pairs_hbm,
    group_hbm,
    local_hbm,
    sizes_hbm,
    rhs_hbm,
    start_hbm,
    self_hbm,
    near_hbm,
    far_hbm,
    pair_ref,
    norm_ref,
    counts,
    pairs,
    groups,
    locals_,
    sizes,
    rhs_ref,
    start_ref,
    self_blk,
    near_blk,
    far_raw,
    left_all,
    right_all,
    onehot,
    row_of,
    field_first,
    field_second,
    beside_first,
    beside_second,
    own_field,
    own_tiles,
    far_back,
    near_back,
    near_in,
    spread,
    core_in,
    x_out,
    x_in,
    z_out,
    z_in,
    y_buf,
    resid,
    stats,
    load_sem,
    send_sem,
    agz_sem,
    agx_sem,
    agy_sem,
    agc_sem,
    rsc_sem,
    rsx_sem,
    rsz_sem,
    y_sem,
    beside_sem,
    near_sem,
    stat_sem,
):
    me = lax.axis_index("clus")
    y = lax.axis_index("pair")
    z = lax.shift_right_logical(me, 3)
    x = lax.bitwise_and(lax.shift_right_logical(me, 1), NX - 1)
    c = lax.bitwise_and(me, NC - 1)

    loads = [
        pltpu.make_async_copy(src, dst, load_sem.at[i])
        for i, (src, dst) in enumerate(
            [
                (counts_hbm, counts),
                (pairs_hbm, pairs),
                (group_hbm, groups),
                (local_hbm, locals_),
                (sizes_hbm, sizes),
                (start_hbm, start_ref),
                (far_hbm, far_raw),
                (near_hbm, near_blk),
                (self_hbm, self_blk),
                (rhs_hbm, rhs_ref),
            ]
        )
    ]
    for load in loads:
        load.start()

    def wrap(value, size):
        return lax.bitwise_and(value, size - 1)

    def dev(zz=None, xx=None, cc=None, yy=None):
        zz = z if zz is None else zz
        xx = x if xx is None else xx
        cc = c if cc is None else cc
        yy = y if yy is None else yy
        return ((zz * NX + xx) * NC + cc, yy)

    def send(src, dst, ssem, rsem, target):
        pltpu.make_async_remote_copy(
            src_ref=src,
            dst_ref=dst,
            send_sem=ssem,
            recv_sem=rsem,
            device_id=target,
            device_id_type=pl.DeviceIdType.MESH,
        ).start()

    def await_bytes(ref, sem):
        pltpu.make_async_copy(ref, ref, sem).wait()

    x_others = [wrap(x + d, NX) for d in (2, 1, 3)]
    x_targets = [dev(xx=o) for o in x_others]
    y_targets = [dev(yy=wrap(y + d, NY)) for d in (2, 1, 3)]
    core = dev(cc=1 - c)
    below = wrap(me + GROUPS - 1, GROUPS)
    above = wrap(me + 1, GROUPS)
    def hops(place):
        dz, dx, dc = place
        return min(dz, NZ - dz) + min(dx, NX - dx) + 0.5 * dc

    places = [(i, j, k) for i in range(NZ) for j in range(NX) for k in range(NC)]
    everyone = [
        dev(zz=wrap(z + i, NZ), xx=wrap(x + j, NX), cc=wrap(c + k, NC))
        for i, j, k in sorted(places, key=hops, reverse=True)
        if i or j or k
    ]
    zx_targets = [
        (dz, dev(zz=wrap(z + dz, NZ), xx=wrap(x + dx, NX)))
        for dz in (4, 3, 5, 2, 6, 1, 7, 0)
        for dx in (2, 1, 3, 0)
        if dz or dx
    ]
    partners = [target for _, target in zx_targets] + y_targets + [core, (below, y), (above, y)]

    barrier = pltpu.get_barrier_semaphore()
    for target in partners:
        pl.semaphore_signal(
            barrier, inc=1, device_id=target, device_id_type=pl.DeviceIdType.MESH
        )

    for load in loads[:6]:
        load.wait()
    lane = lax.broadcasted_iota(jnp.int32, (RHS, PAD), 1)
    valid = [(lane < sizes[i]).astype(F32) for i in range(CG)]
    near_live = counts[0, 0]
    far_live = counts[0, 1]


    def far_place(k):
        group = groups[0, k]
        return (
            lax.bitwise_and(group, 1) * HALF
            + lax.shift_right_logical(group, 1) * CG
            + locals_[1, k]
        )

    def far_tile(k):
        group = groups[0, k]
        return (
            lax.bitwise_and(group, 1) * NZ + lax.shift_right_logical(group, 3),
            locals_[1, k],
            lax.bitwise_and(lax.shift_right_logical(group, 1), NX - 1),
        )

    diagonal = (
        lax.broadcasted_iota(jnp.int32, (CHUNK * RHS, WIDE), 0) // RHS
        == lax.broadcasted_iota(jnp.int32, (CHUNK * RHS, WIDE), 1) // RANK
    )

    def far_to_near(j):
        odd = j % 2
        return wrap(z + NZ // 2 + (1 - 2 * odd) * ((j + 1) // 2), NZ)

    def prepare():
        slot = lax.broadcasted_iota(jnp.int32, (RHS, WIDE), 1) // RANK

        def rows_step(chunk, carry):
            table = jnp.full((RHS, WIDE), -1, jnp.int32)
            for s in range(CHUNK):
                k = chunk * CHUNK + s
                row = jnp.where(k < far_live, locals_[0, k], -1)
                table = jnp.where(slot == s, row, table)
            row_of[chunk] = table
            return carry

        lax.fori_loop(0, CHUNKS, rows_step, 0)

        wide = lax.broadcasted_iota(jnp.int32, (RHS, FAR * RHS), 1)
        slot_of = wide // RHS

        def place_step(step, table):
            for s in range(8):
                k = step * 8 + s
                table = jnp.where(slot_of == k, far_place(k), table)
            return table

        table = lax.fori_loop(
            0, FAR // 8, place_step, jnp.full((RHS, FAR * RHS), -1, jnp.int32)
        )
        same = lax.broadcasted_iota(jnp.int32, (RHS, FAR * RHS), 0) == wide % RHS
        table = jnp.where(same, table, -1)

        def onehot_step(step, carry):
            for s in range(4):
                i = step * 4 + s
                two = jnp.concatenate(
                    [
                        jnp.where(table == 2 * i, 1.0, 0.0),
                        jnp.where(table == 2 * i + 1, 1.0, 0.0),
                    ],
                    axis=0,
                ).astype(BF16)
                onehot[pl.ds(pl.multiple_of(i * 16, 16), 16), :] = two
            return carry

        lax.fori_loop(0, GROUPS * CG // 8, onehot_step, 0)
        loads[6].wait()

        def factor_step(chunk, carry):
            rows = pl.ds(pl.multiple_of(chunk * WIDE, WIDE), WIDE)
            raw = far_raw[pl.ds(chunk * CHUNK, CHUNK)].astype(F32)
            left_all[rows, :] = raw[:, 0].reshape(WIDE, PAD).astype(BF16)
            right_all[rows, :] = raw[:, 1].reshape(WIDE, PAD).astype(BF16)
            return carry

        lax.fori_loop(0, CHUNKS, factor_step, 0)

    def apply_operator(a, values):
        field = (field_first, field_second)[a]
        beside = (beside_first, beside_second)[a]
        for i in range(CG):
            packed = values[i].astype(BF16).astype(F32)
            low = values[i] - packed if a else jnp.zeros_like(packed)
            own_field[a, i] = jnp.concatenate([packed, low], axis=0)
            own_tiles[a, i] = fold(packed).astype(BF16)

        def send_field():
            for dz, to in zx_targets:
                if dz in NEAR_Z:
                    own, here = own_tiles.at[a], field.at[c * NZ + z, :, x]
                    send(own, here, send_sem.at[a, 0], agx_sem.at[a, z], to)
                else:
                    own, here = own_tiles.at[a, y], field.at[c * NZ + z, y, x]
                    send(own, here, send_sem.at[a, 2], agx_sem.at[a, z], to)
            for slot, target in ((0, above), (1, below)):
                to = beside.at[pl.ds(slot * CG, CG)]
                send(own_tiles.at[a], to, send_sem.at[a, 7], beside_sem.at[a], (target, y))
            field[c * NZ + z, :, x] = own_tiles[a]

        def far_out():
            own_rows = jnp.concatenate(
                [own_field[a, i, 0:RHS] for i in range(CG)], axis=0
            ).astype(BF16)

            def back_step(chunk, carry):
                rows = pl.ds(pl.multiple_of(chunk * WIDE, WIDE), WIDE)
                every = dot_nt(own_rows, left_all[rows, :])
                table = row_of[chunk]
                coef = jnp.zeros((RHS, WIDE), F32)
                for i in range(CG):
                    coef = coef + jnp.where(
                        table == i, every[i * RHS : (i + 1) * RHS], 0.0
                    )
                tall = jnp.concatenate([coef] * CHUNK, axis=0)
                tall = jnp.where(diagonal, tall, 0.0).astype(BF16)
                out = dot_nn(tall, right_all[rows, :])
                at = pl.ds(pl.multiple_of(chunk * CHUNK * RHS, CHUNK * RHS), CHUNK * RHS)
                far_back[a, at, :] = out.astype(BF16)
                return carry

            lax.fori_loop(0, CHUNKS, back_step, 0, unroll=True)

        def near_out():
            near_back[a] = jnp.zeros((3 * CG, RHS, PAD), F32)

            def near_back_step(step, carry):
                for s in range(UNROLL):
                    k = step * UNROLL + s
                    live = jnp.where(k < near_live, 1.0, 0.0)
                    out = dot_nn(own_field[a, pairs[0, k]].astype(BF16), near_blk[k])
                    out = out[:RHS] + out[RHS:]
                    column = pairs[1, k]
                    for j in range(3 * CG):
                        near_back[a, j] += out * jnp.where(column == j, live, 0.0)
                return carry

            lax.fori_loop(0, NEAR // UNROLL, near_back_step, 0)

        def spread_part(half, zz):
            block = half * NZ + zz
            rows = pl.ds(pl.multiple_of(block * PART * RHS, PART * RHS), PART * RHS)
            out = dot_nn(onehot[rows, :], far_back[a])
            return fold(out.reshape(PART, RHS, PAD))

        def theirs_step(j, carry):
            zz = far_to_near(j)
            spread[a, zz] = spread_part(1 - c, zz).astype(BF16)
            return carry

        def to_core_step(j, carry):
            zz = far_to_near(j)
            send(
                spread.at[a, zz], core_in.at[a, zz], send_sem.at[a, 1], rsc_sem.at[a, zz], core
            )
            return carry

        def ours_step(j, carry):
            zz = far_to_near(j)
            await_bytes(core_in.at[a, zz], rsc_sem.at[a, zz])
            total = spread_part(c, zz) + core_in[a, zz].astype(F32)
            x_out[a, zz] = total.reshape(NX, CG, 16, 128).astype(BF16)
            for o in x_others:
                send(
                    x_out.at[a, zz, o],
                    x_in.at[a, zz, x],
                    send_sem.at[a, 4],
                    rsx_sem.at[a, zz],
                    dev(xx=o),
                )
            return carry

        def along_y(d):
            zz = wrap(z + NZ - d, NZ)
            run = field.at[c * NZ + zz, y]
            await_bytes(run, agx_sem.at[a, zz])
            for target in y_targets:
                send(run, run, send_sem.at[a, 10], agy_sem.at[a, zz], target)

        def to_other_core(d):
            zz = wrap(z + NZ - d, NZ)
            slab = field.at[c * NZ + zz]
            if d in NEAR_Z:
                await_bytes(slab if d else field.at[0, pl.ds(0, NX - 1)], agx_sem.at[a, zz])
            else:
                await_bytes(field.at[0, pl.ds(0, NY - 1)], agy_sem.at[a, zz])
            send(slab, slab, send_sem.at[a, 3], agc_sem.at[a], core)

        if a == 0:
            prepare()
            far_out()
            lax.fori_loop(0, NZ, theirs_step, 0, unroll=True)
            pl.semaphore_wait(barrier, len(partners))
            send_field()
            lax.fori_loop(0, NZ, to_core_step, 0, unroll=True)
            lax.fori_loop(0, NZ, ours_step, 0, unroll=True)
        else:
            send_field()
            far_out()

            def both(j, carry):
                return to_core_step(j, theirs_step(j, carry))

            def all_three(j, carry):
                return ours_step(j, both(j + LAG, carry))

            lax.fori_loop(0, LAG, both, 0, unroll=True)
            lax.fori_loop(0, NZ - LAG, all_three, 0, unroll=True)
            lax.fori_loop(NZ - LAG, NZ, ours_step, 0, unroll=True)
        if a == 0:
            loads[7].wait()
            loads[8].wait()
        order = [0, 1, 7, 2, 6, 3, 5, 4]
        near_out()
        for first, slot, target in ((0, 1, below), (2 * CG, 0, above)):
            send(
                near_back.at[a, pl.ds(first, CG)],
                near_in.at[a, slot],
                send_sem.at[a, 8],
                near_sem.at[a],
                (target, y),
            )
        for d in (1, 7, 2, 6):
            along_y(d)
        await_bytes(beside, beside_sem.at[a])

        def near_step(step, sums):
            for s in range(UNROLL):
                k = step * UNROLL + s
                column = pairs[1, k]
                inside = lax.bitwise_and(column, CG - 1)
                own = jnp.logical_and(column >= CG, column < 2 * CG)
                tile = unfold(beside[jnp.where(column < CG, 0, CG) + inside].astype(F32))
                tile = jnp.concatenate([tile, jnp.zeros_like(tile)], axis=0)
                tile = jnp.where(own, own_field[a, inside], tile).astype(BF16)
                out = dot_nt(tile, near_blk[k])
                out = out[:RHS] + out[RHS:]
                row = pairs[0, k]
                live = jnp.where(k < near_live, 1.0, 0.0)
                sums = tuple(
                    sums[i] + out * jnp.where(row == i, live, 0.0) for i in range(CG)
                )
            return sums

        sums = tuple(near_back[a, CG + i] for i in range(CG))
        sums = lax.fori_loop(0, NEAR // UNROLL, near_step, sums)
        for d in (3, 5, 4):
            along_y(d)
        to_other_core(0)

        def x_sum_step(j):
            zz = far_to_near(j)
            await_bytes(x_in.at[a, zz, pl.ds(0, NX - 1)], rsx_sem.at[a, zz])
            x_in[a, zz, x] = x_out[a, zz, x]
            total = x_in[a, zz, 0].astype(F32)
            for o in range(1, NX):
                total = total + x_in[a, zz, o].astype(F32)
            z_out[a, zz] = total.astype(BF16)
            if j < NZ - 1:
                send(
                    z_out.at[a, zz], z_in.at[a, z], send_sem.at[a, 5], rsz_sem.at[a], dev(zz=zz)
                )

        for j in range(NZ):
            x_sum_step(j)
        for d in order[1:]:
            to_other_core(d)
        if a:
            share(0, [total_of([resid[i] * resid[i] for i in range(CG)])])

        await_bytes(field.at[pl.ds(0, NZ)], agc_sem.at[a])

        def forth_step(chunk, total):
            rows = pl.ds(pl.multiple_of(chunk * WIDE, WIDE), WIDE)
            tiles = [
                unfold(field[far_tile(chunk * CHUNK + s)].astype(F32))
                for s in range(CHUNK)
            ]
            tall = jnp.concatenate(tiles, axis=0).astype(BF16)
            every = jnp.where(diagonal, dot_nt(tall, right_all[rows, :]), 0.0)
            coef = jnp.sum(every.reshape(CHUNK, RHS, WIDE), axis=0)
            table = row_of[chunk]
            four = jnp.concatenate(
                [jnp.where(table == i, coef, 0.0) for i in range(CG)], axis=0
            )
            return total + dot_nn(four.astype(BF16), left_all[rows, :])

        far_rows = lax.fori_loop(
            0, CHUNKS, forth_step, jnp.zeros((CG * RHS, PAD), F32), unroll=True
        )
        self_out = dot_nt(own_field[a, y].astype(BF16), self_blk[0])
        self_out = self_out[:RHS] + self_out[RHS:]

        await_bytes(near_in.at[a], near_sem.at[a])
        ready = [
            near_in[a, 0, i]
            + near_in[a, 1, i]
            + sums[i]
            + far_rows[i * RHS : (i + 1) * RHS]
            + self_out * jnp.where(y == i, 1.0, 0.0)
            for i in range(CG)
        ]
        await_bytes(z_in.at[a, pl.ds(0, NZ - 1)], rsz_sem.at[a])
        z_in[a, z] = z_out[a, z]
        for i in range(CG):
            come = z_in[a, 0, i].astype(F32)
            for j in range(1, NZ):
                come = come + z_in[a, j, i].astype(F32)
            y_buf[a, y, i] = ready[i] + unfold(come)
            part = y_buf.at[a, y, i]
            for target in y_targets:
                send(part, part, send_sem.at[a, 6], y_sem.at[a], target)
        if a:
            meanwhile()
        await_bytes(y_buf.at[a, pl.ds(0, NY - 1)], y_sem.at[a])
        return [
            valid[i] * (y_buf[a, 0, i] + y_buf[a, 1, i] + y_buf[a, 2, i] + y_buf[a, 3, i])
            for i in range(CG)
        ]

    sub = lax.broadcasted_iota(jnp.int32, (RHS, 128), 0)
    lane = lax.broadcasted_iota(jnp.int32, (RHS, 128), 1)

    def share(s, columns):
        spots = [
            jnp.where(lane == sub + p * RHS, column, 0.0) for p, column in enumerate(columns)
        ]
        row = functools.reduce(lambda p, q: p + q, spots)
        stats[s, pl.ds(me, 1)] = jnp.sum(row, axis=0, keepdims=True)
        part = stats.at[s, pl.ds(me, 1)]

        for target in everyone:
            send(part, part, send_sem.at[s, 9], stat_sem.at[s], target)

    def shared(s):
        await_bytes(stats.at[s, pl.ds(0, GROUPS - 1)], stat_sem.at[s])
        return stats[s]

    def column_of(row):
        tall = jnp.where(lane == sub, jnp.broadcast_to(row, (RHS, 128)), 0.0)
        return jnp.sum(tall, axis=1, keepdims=True)

    def total_of(tiles):
        return jnp.sum(
            functools.reduce(lambda p, q: p + q, tiles), axis=1, keepdims=True
        )

    def cut(ref, i):
        return ref[:, i * PAD : (i + 1) * PAD]

    initial = [cut(start_ref, i) * valid[i] for i in range(CG)]
    image = apply_operator(0, initial)
    loads[9].wait()
    for i in range(CG):
        resid[i] = cut(rhs_ref, i) * valid[i] - image[i]
    known = {}

    def meanwhile():
        square = jnp.sum(shared(0), axis=0, keepdims=True)
        known["norm"] = jnp.sqrt(square / PANELS + EPSILON)
        column = column_of(known["norm"])
        known["column"] = column
        known["basis"] = [resid[i] / column for i in range(CG)]
        known["size"] = total_of([v * v for v in known["basis"]])

    image = apply_operator(1, [resid[i] for i in range(CG)])
    start_norm, basis, size = known["norm"], known["basis"], known["size"]
    image = [image[i] / known["column"] for i in range(CG)]
    inner = total_of([basis[i] * image[i] for i in range(CG)])
    centre = ratio(inner, size)
    rest = [image[i] - centre * basis[i] for i in range(CG)]
    share(1, [inner, size, total_of([rest[i] * rest[i] for i in range(CG)])])

    inner = shared(1)
    size = pltpu.roll(inner, 128 - RHS, 1)
    rest = pltpu.roll(inner, 128 - 2 * RHS, 1)
    inner_all = jnp.sum(inner, axis=0, keepdims=True)
    h_diag = inner_all / PANELS
    below_square = jnp.sum(about(inner, size, rest, h_diag), axis=0, keepdims=True)
    h_below = jnp.sqrt(jnp.maximum(below_square, 0.0) / PANELS + EPSILON)
    denominator = h_diag * h_diag + h_below * h_below
    step_size = column_of(start_norm * h_diag / denominator)
    norm_ref[...] = start_norm * h_below / jnp.sqrt(denominator)
    diag_column = column_of(h_diag)
    below_column = column_of(h_below)
    for i in range(CG):
        pair_ref[0, :, i * PAD : (i + 1) * PAD] = (
            cut(start_ref, i) * valid[i] + step_size * basis[i]
        )
        pair_ref[1, :, i * PAD : (i + 1) * PAD] = (
            image[i] - diag_column * basis[i]
        ) / below_column

    for a in range(2):
        field = (field_first, field_second)[a]
        await_bytes(spread.at[a], send_sem.at[a, 1])
        await_bytes(field.at[0, pl.ds(0, NX - 1)], send_sem.at[a, 0])
        await_bytes(field.at[pl.ds(0, 1), pl.ds(0, CG)], send_sem.at[a, 2])
        await_bytes(field.at[0, pl.ds(0, 3)], send_sem.at[a, 2])
        await_bytes(field.at[pl.ds(0, NZ - 1), pl.ds(0, NY - 1)], send_sem.at[a, 10])
        await_bytes(field.at[pl.ds(0, NZ)], send_sem.at[a, 3])
        await_bytes(x_in.at[a, pl.ds(0, NZ), pl.ds(0, NX - 1)], send_sem.at[a, 4])
        await_bytes(z_in.at[a, pl.ds(0, NZ - 1)], send_sem.at[a, 5])
        await_bytes(y_buf.at[a, pl.ds(0, NY - 1)], send_sem.at[a, 6])
        await_bytes(field.at[0, pl.ds(0, 2)], send_sem.at[a, 7])
        await_bytes(near_in.at[a], send_sem.at[a, 8])
        await_bytes(stats.at[a, pl.ds(0, GROUPS - 1)], send_sem.at[a, 9])


def local(
    right_side,
    start,
    cluster_sizes,
    self_blocks,
    near_blocks,
    near_pairs,
    far_factors,
    far_group,
    far_local,
    block_counts,
):
    vmem = pl.BlockSpec(memory_space=pltpu.VMEM)
    hbm = pl.BlockSpec(memory_space=pl.ANY)
    dma = pltpu.SemaphoreType.DMA
    wide = (RHS, CG * PAD)
    both, norm = pl.pallas_call(
        kernel,
        out_shape=(
            jax.ShapeDtypeStruct((2,) + wide, F32),
            jax.ShapeDtypeStruct((1, 128), F32),
        ),
        in_specs=[hbm] * 10,
        out_specs=(vmem, vmem),
        scratch_shapes=[
            pltpu.SMEM((1, 2), jnp.int32),
            pltpu.SMEM((2, NEAR), jnp.int32),
            pltpu.SMEM((1, FAR), jnp.int32),
            pltpu.SMEM((2, FAR), jnp.int32),
            pltpu.SMEM((CG,), jnp.int32),
            pltpu.VMEM(wide, F32),
            pltpu.VMEM(wide, F32),
            pltpu.VMEM((1, PAD, PAD), BF16),
            pltpu.VMEM((NEAR, PAD, PAD), BF16),
            pltpu.VMEM((FAR, 2, RANK, PAD), BF16),
            pltpu.VMEM((FAR * RANK, PAD), BF16),
            pltpu.VMEM((FAR * RANK, PAD), BF16),
            pltpu.VMEM((GROUPS * CG * RHS, FAR * RHS), BF16),
            pltpu.VMEM((CHUNKS, RHS, WIDE), jnp.int32),
            pltpu.VMEM((NC * NZ, CG, NX, 16, 128), BF16),
            pltpu.VMEM((NC * NZ, CG, NX, 16, 128), BF16),
            pltpu.VMEM((2 * CG, 16, 128), BF16),
            pltpu.VMEM((2 * CG, 16, 128), BF16),
            pltpu.VMEM((2, CG, 2 * RHS, PAD), F32),
            pltpu.VMEM((2, CG, 16, 128), BF16),
            pltpu.VMEM((2, FAR * RHS, PAD), BF16),
            pltpu.VMEM((2, 3 * CG, RHS, PAD), F32),
            pltpu.VMEM((2, 2, CG, RHS, PAD), F32),
            pltpu.VMEM((2, NZ, PART, 16, 128), BF16),
            pltpu.VMEM((2, NZ, PART, 16, 128), BF16),
            pltpu.VMEM((2, NZ, NX, CG, 16, 128), BF16),
            pltpu.VMEM((2, NZ, NX, CG, 16, 128), BF16),
            pltpu.VMEM((2, NZ, CG, 16, 128), BF16),
            pltpu.VMEM((2, NZ, CG, 16, 128), BF16),
            pltpu.VMEM((2, NY, CG, RHS, PAD), F32),
            pltpu.VMEM((CG, RHS, PAD), F32),
            pltpu.VMEM((2, GROUPS, 128), F32),
            dma((10,)),
            dma((2, 11)),
            dma((2, NZ - 1)),
            dma((2, NZ)),
            dma((2, NZ)),
            dma((2,)),
            dma((2, NZ)),
            dma((2, NZ)),
            dma((2,)),
            dma((2,)),
            dma((2,)),
            dma((2,)),
            dma((2,)),
        ],
        compiler_params=pltpu.CompilerParams(
            collective_id=0, has_side_effects=True, vmem_limit_bytes=60 * 1024 * 1024
        ),
    )(
        block_counts,
        near_pairs.T,
        far_group.T,
        far_local.T,
        cluster_sizes,
        right_side,
        start,
        self_blocks,
        near_blocks,
        far_factors,
    )
    return both[0], both[1], norm[0, :RHS]


def solution(mesh):
    in_specs = (
        P(None, "clus"),
        P(None, "clus"),
        P("clus"),
        P(("clus", "pair"), None, None),
        P(("clus", "pair"), None, None),
        P(("clus", "pair"), None),
        P(("clus", "pair"), None, None, None),
        P(("clus", "pair"), None),
        P(("clus", "pair"), None),
        P(("clus", "pair"), None),
    )
    out_specs = (P(None, "clus"), P(None, "clus"), P())
    return jax.shard_map(local, mesh=mesh, in_specs=in_specs, out_specs=out_specs, check_vma=False)
```
